256 devices in a mesh: segment: 8 (over x, core), expert: 32 (over y, z).
Axes of the slice: x: 4, y: 4, z: 8, core: 2. Of those that a mesh axis runs over, the one named last changes fastest.
Arguments:
- tokens: bfloat16 [8, 4096, 7168], P('segment', 'expert'), may hold values from -6 to 6
- entering: bfloat16 [4096, 7168], P('expert'), may hold values from -6 to 6
- norm_gain: float32 [8, 7168], P('segment'), may hold values from 0.1 to 1.9
- gate_up: bfloat16 [8, 32, 896, 8, 2, 128], P('segment', 'expert'), may hold values from -0.0625 to 0.0625
- down_proj: bfloat16 [8, 32, 1024, 896], P('segment', 'expert'), may hold values from -0.1875 to 0.1875
- expert_ids: int32 [8, 4096, 1], P('segment', 'expert'), may hold values from 0 to 3; in each aligned block of 128 rows (0 to 127, 128 to 255, ..., all dimensions but the last counted through in order) at most 36 rows name the same one
- gate_weights: float32 [8, 4096, 1], P('segment', 'expert'), may hold values from 0.5 to 2
Outputs:
- segment_outputs: bfloat16 [2, 8, 4096, 7168], P(None, 'segment', 'expert')
The draws below stay inside these ranges and needn't reach their ends.
Inputs may be any that keep to these rules, and one draw needn't show every extreme that they name: `expert_ids`: among the 128 tokens that one device holds in one segment, at most 36 name the same expert, and in some of these blocks one expert is named by exactly 36.
All inputs are finite; a program needn't handle non-finite values.
Results may differ from the reference program's by a relative error of at most 0.008.
Values may be sent and summed in bfloat16 or wider, within the bound.
No kernel may reach another device: no remote copies, remote signals or barrier semaphores. Data moves between devices by JAX's collectives and lax.ppermute only.
A program may use at most 128 MiB of HBM per device.

```python
import math
import jax
import jax.numpy as jnp
import numpy as np
from jax import lax

D = 7168
FF = 1024
SPLIT = 8
TOP = 1
TOK_DEV = 128
EXPERTS = 4
CAP = 36
TOKENS = 4096
DS = 896
FS = 128
N_SEGMENT = 8
N_EXPERT = 32


def block_scale(stream_key, dims, split, smallest, top_value):
    def one(position, shards_of):
        draws = jax.random.uniform(jax.random.fold_in(jax.random.fold_in(stream_key, 6), position), (shards_of,), jnp.float32, smallest / len(split), top_value / len(split))
        return jnp.repeat(jnp.exp(draws), dims[position] // shards_of).reshape((-1,) + (1,) * (len(dims) - position - 1))

    gain = one(*split[0])
    for cut in split[1:]:
        gain = gain * one(*cut)
    return gain


def shared_out(stream_key, own, number, rows, count, top, most, lean):
    ranking = jax.random.permutation(stream_key, count)
    crowded, common = shares(count, rows * top, most, lean, True), shares(count, rows * top, most, lean, False)
    places = jnp.arange(count)

    def named(lengths, rotation):
        used = int((lengths > 0).sum())
        fixed = max(1, used // 4)
        moved = fixed + (places - fixed + rotation * (used - fixed)) % max(1, count - fixed)
        return jnp.zeros((count,), jnp.int32).at[ranking[jnp.where(places < fixed, places, moved)]].set(jnp.asarray(lengths, jnp.int32))

    lengths = jnp.where(number % 4 == 0, named(crowded, number // 4), named(common, number - number // 4 - 1))
    mixed = jax.random.permutation(jax.random.fold_in(own, 3), count)
    donor, taker = mixed[0:count // 2 * 2:2], mixed[1:count // 2 * 2:2]
    room = jnp.minimum(lengths[donor] - 1, most - lengths[taker]) // 2
    room = jnp.where((donor == ranking[0]) | (taker == ranking[0]) | (lengths[taker] == 0), 0, jnp.maximum(room, 0))
    moved = jax.random.randint(jax.random.fold_in(own, 4), (count // 2,), 0, 1 << 20) % (room + 1)
    lengths = lengths.at[donor].add(-moved).at[taker].add(moved)
    items = jnp.searchsorted(jnp.cumsum(lengths), jnp.arange(rows * top), side="right").astype(jnp.int32)
    listing = items.reshape(top, rows).T
    listing = listing[jax.random.permutation(jax.random.fold_in(own, 1), rows)]
    rotation = jax.random.randint(jax.random.fold_in(own, 2), (rows, 1), 0, top)
    return jnp.take_along_axis(listing, (jnp.arange(top)[None, :] + rotation) % top, axis=1)


def shares(amount, total, reach, lean, full):
    portions = [(1 << 20) // math.isqrt(rank ** lean) + 1 for rank in range(1, amount + 1)]
    largest = reach if full else min(reach, max(-(-total // amount), total * portions[0] // sum(portions)))
    least = 1 if total - largest >= amount - 1 else 0
    given, rest = [largest] + [least] * (amount - 1), total - largest - least * (amount - 1)
    while rest > 0:
        free = [i for i in range(1, amount) if given[i] < largest] or [i for i in range(1, amount) if given[i] < reach]
        pool, budget = sum([portions[i] for i in free]), rest
        for i in free:
            extra = min(reach - given[i], max(1, budget * portions[i] // pool), rest)
            given[i] = given[i] + extra
            rest = rest - extra
    return np.array(given)


def noise(own_key, extent, spread, limit, pieces=(), held_as=jnp.bfloat16):
    gain = block_scale(own_key, extent, pieces, -0.22, 0.18) if pieces else 1.0
    result = jax.random.normal(own_key, extent, jnp.float32) * spread * gain
    return jnp.minimum(jnp.maximum(result, -limit), limit).astype(held_as)


def setup_inputs(seed: int = 0) -> dict:
    keys = jax.random.split(jax.random.key(seed), 8)
    tokens = noise(keys[0], (N_SEGMENT, TOKENS, D), 1.0, 6.0, ((0, 8), (1, 32)))
    entering = noise(keys[1], (TOKENS, D), 1.0, 6.0, ((0, 32),))
    norm_gain = jnp.clip(1.0 + 0.18 * jax.random.normal(keys[2], (N_SEGMENT, D), jnp.float32), 0.1, 1.9)
    gate_up = noise(keys[3], (N_SEGMENT, EXPERTS * SPLIT, DS, SPLIT, 2, FS), D ** -0.5, 0.0625, ((0, 8), (1, 32)))
    down_proj = noise(keys[4], (N_SEGMENT, EXPERTS * SPLIT, FF, DS), FF ** -0.5, 0.1875, ((0, 8), (1, 32)))
    expert_ids_keys = jax.random.split(jax.random.fold_in(keys[5], 1), N_SEGMENT * TOKENS // TOK_DEV)
    expert_ids_turns = jax.random.permutation(jax.random.fold_in(keys[5], 3), N_SEGMENT * TOKENS // TOK_DEV)
    expert_ids = jax.vmap(lambda own, number: shared_out(jax.random.fold_in(keys[5], 2), own, number, TOK_DEV, EXPERTS, TOP, CAP, 2))(expert_ids_keys, expert_ids_turns).reshape((N_SEGMENT, TOKENS, TOP))
    gate_weights = jnp.clip(jnp.exp(math.log(2.0) - 1.3862944 * jax.random.uniform(keys[6], (N_SEGMENT, TOKENS, TOP), jnp.float32) ** block_scale(keys[6], (N_SEGMENT, TOKENS, TOP), ((0, 8), (1, 32)), -0.2, 0.2)), 0.5, 2.0)
    return dict(tokens=tokens, entering=entering, norm_gain=norm_gain, gate_up=gate_up, down_proj=down_proj, expert_ids=expert_ids, gate_weights=gate_weights)


EPSILON = 1e-06

def apply_layer(stream, segment_num, norm_gain, gate_up, down_proj, expert_ids, gate_weights):
    limit_rows = N_EXPERT * CAP
    values = stream.astype(jnp.float32)
    mean_sq = lax.optimization_barrier(jnp.mean(values * values, axis=-1, keepdims=True))
    normed = (values * lax.rsqrt(mean_sq + EPSILON) * norm_gain[segment_num]).astype(jnp.bfloat16)
    flat_ids = expert_ids[segment_num].reshape(TOKENS * TOP)
    flat_weights = gate_weights[segment_num].reshape(TOKENS * TOP)
    accumulated = jnp.zeros((TOKENS, D), jnp.float32)
    for expert_num in range(EXPERTS):
        matches = flat_ids == expert_num
        positions, = jnp.nonzero(matches, size=limit_rows, fill_value=0)
        is_valid = jnp.arange(limit_rows) < jnp.sum(matches.astype(jnp.int32))
        token_num = (positions // TOP).astype(jnp.int32)
        picked = normed[token_num]
        first_lane = expert_num * SPLIT
        gate_block = gate_up[segment_num, first_lane:first_lane + SPLIT].reshape(D, 2 * FF)
        projected = jnp.dot(picked, gate_block, preferred_element_type=jnp.float32)
        projected = projected.reshape(limit_rows, SPLIT, 2, FS)
        gate_part = projected[:, :, 0, :].reshape(limit_rows, FF)
        up_part = projected[:, :, 1, :].reshape(limit_rows, FF)
        hidden = (jax.nn.silu(gate_part) * up_part).astype(jnp.bfloat16)
        down_block = jnp.transpose(down_proj[segment_num, first_lane:first_lane + SPLIT], (1, 0, 2)).reshape(FF, D)
        expert_out = jnp.dot(hidden, down_block, preferred_element_type=jnp.float32).astype(jnp.bfloat16)
        row_scale = jnp.where(is_valid, flat_weights[positions], jnp.zeros((), jnp.float32))
        accumulated = accumulated.at[token_num].add(expert_out.astype(jnp.float32) * row_scale[:, None])
    return (values + accumulated).astype(jnp.bfloat16)

def reference(tokens, entering, norm_gain, gate_up, down_proj, expert_ids, gate_weights):
    first_tick = []
    for segment_num in range(N_SEGMENT):
        first_tick.append(apply_layer(tokens[segment_num], segment_num, norm_gain, gate_up, down_proj, expert_ids, gate_weights))
    second_tick = []
    for segment_num in range(N_SEGMENT):
        source = entering if segment_num == 0 else first_tick[segment_num - 1]
        second_tick.append(apply_layer(source, segment_num, norm_gain, gate_up, down_proj, expert_ids, gate_weights))
    return jnp.stack([jnp.stack(first_tick), jnp.stack(second_tick)])
```

```python
import jax
import jax.numpy as jnp
from jax import lax
from jax.sharding import Mesh, PartitionSpec as P

EPSILON = 1e-06


def shifted(value, axis, by):
    count = lax.axis_size(axis)
    return lax.ppermute(value, axis, [(i, (i + by) % count) for i in range(count)])


def passed_along(shard, axis, by):
    count = lax.axis_size(axis)
    pairs = [(i, i + by) for i in range(count) if 0 <= i + by < count]
    return lax.ppermute(shard, axis, pairs)


def rms_normed(stream, gain_row):
    values = stream.astype(jnp.float32)
    mean_sq = jnp.mean(values * values, axis=-1, keepdims=True)
    return (values * lax.rsqrt(mean_sq + EPSILON) * gain_row).astype(jnp.bfloat16)


def per_device(tokens, entering, norm_gain, gate_up, down_proj, expert_ids, gate_weights):
    split = lax.axis_size("z")
    groups = lax.axis_size("y")
    segment_index = lax.axis_index("segment")
    place = lax.axis_index("z")
    tok_rows, model_width = entering.shape
    slot_cap = 9 * tok_rows // (8 * groups)
    piece_width = model_width // split
    hidden_width = down_proj.shape[2]
    flat_ids = expert_ids[0].reshape(tok_rows)
    member = (flat_ids[:, None] == jnp.arange(groups, dtype=jnp.int32)[None, :]).astype(jnp.int32)
    slot_of = jnp.sum((jnp.cumsum(member, axis=0) - 1) * member, axis=1)
    target = flat_ids * slot_cap + slot_of
    pick_table = (
        (jnp.arange(groups * slot_cap, dtype=jnp.int32)[:, None] == target[None, :])
        .astype(jnp.bfloat16)
        .reshape(groups, slot_cap, tok_rows)
    )
    token_weight = gate_weights[0][:, 0]
    weights_in = gate_up[0, 0].reshape(piece_width, 2 * hidden_width)
    weights_out = down_proj[0, 0]
    half = hidden_width
    far = split // 2

    def moe_layer(stream):
        normed = rms_normed(stream, norm_gain[0])
        outgoing = jnp.einsum(
            "gcr,rjp->jgcp",
            pick_table,
            normed.reshape(tok_rows, split, piece_width),
            preferred_element_type=jnp.float32,
        )
        outgoing = outgoing.astype(jnp.bfloat16).reshape(split * groups, slot_cap, piece_width)
        arrived = lax.all_to_all(outgoing, ("z", "y"), split_axis=0, concat_axis=0, tiled=True)
        arrived = arrived.reshape(split, groups * slot_cap, piece_width)

        def partial_sums(offset):
            rows = lax.dynamic_index_in_dim(arrived, (place + offset) % split, 0, False)
            return jnp.dot(rows, weights_in, preferred_element_type=jnp.float32)

        opposite = partial_sums(far).astype(jnp.bfloat16)
        low_up, high_down = opposite[:, :half], opposite[:, half:]
        high_up = low_down = None
        for step in range(far - 1, 0, -1):
            low_up = shifted(low_up, "z", 1)
            high_down = shifted(high_down, "z", -1)
            if high_up is not None:
                high_up = shifted(high_up, "z", 1)
                low_down = shifted(low_down, "z", -1)
            ahead, behind = partial_sums(step), partial_sums(-step)
            low_up = (low_up.astype(jnp.float32) + ahead[:, :half]).astype(jnp.bfloat16)
            high_down = (high_down.astype(jnp.float32) + behind[:, half:]).astype(jnp.bfloat16)
            if high_up is None:
                high_up = ahead[:, half:].astype(jnp.bfloat16)
                low_down = behind[:, :half].astype(jnp.bfloat16)
            else:
                high_up = (high_up.astype(jnp.float32) + ahead[:, half:]).astype(jnp.bfloat16)
                low_down = (low_down.astype(jnp.float32) + behind[:, :half]).astype(jnp.bfloat16)
        low_up, high_up = shifted(low_up, "z", 1), shifted(high_up, "z", 1)
        low_down, high_down = shifted(low_down, "z", -1), shifted(high_down, "z", -1)
        own = partial_sums(0)
        low = own[:, :half] + low_up.astype(jnp.float32) + low_down.astype(jnp.float32)
        high = own[:, half:] + high_up.astype(jnp.float32) + high_down.astype(jnp.float32)

        def activated(sums):
            pairs = sums.reshape(groups * slot_cap, -1, 2, 128)
            return (jax.nn.silu(pairs[:, :, 0]) * pairs[:, :, 1]).astype(jnp.bfloat16).reshape(
                groups * slot_cap, half // 2
            )

        hidden = jnp.concatenate([activated(low), activated(high)], axis=1)
        results = jnp.zeros((split, groups * slot_cap, piece_width), jnp.bfloat16)

        def projected(results, rows, offset):
            block = jnp.dot(rows, weights_out, preferred_element_type=jnp.float32)
            return lax.dynamic_update_index_in_dim(
                results, block.astype(jnp.bfloat16), (place + offset) % split, 0
            )

        from_below = from_above = hidden
        results = projected(results, hidden, 0)
        for step in range(1, far):
            from_below = shifted(from_below, "z", 1)
            from_above = shifted(from_above, "z", -1)
            results = projected(results, from_below, -step)
            results = projected(results, from_above, step)
        left = shifted(from_below[:, : half // 2], "z", 1)
        right = shifted(from_above[:, half // 2 :], "z", -1)
        results = projected(results, jnp.concatenate([left, right], axis=1), far)
        returned = lax.all_to_all(
            results.reshape(split * groups, slot_cap, piece_width),
            ("z", "y"),
            split_axis=0,
            concat_axis=0,
            tiled=True,
        )
        returned = returned.reshape(split, groups, slot_cap, piece_width)
        selected = jnp.einsum(
            "gcr,jgcp->rjp", pick_table, returned, preferred_element_type=jnp.float32
        )
        weighted = selected * token_weight[:, None, None]
        return (stream.astype(jnp.float32) + weighted.reshape(tok_rows, model_width)).astype(
            jnp.bfloat16
        )

    first_result = moe_layer(tokens[0])
    passed = passed_along(first_result, "segment", 1)
    second_input = jnp.where(segment_index == 0, entering, passed)
    second_result = moe_layer(second_input)
    return jnp.stack([first_result, second_result])[:, None]


def solution(mesh):
    segments, experts = mesh.devices.shape
    split = 8
    fine = Mesh(mesh.devices.reshape(segments, experts // split, split), ("segment", "y", "z"))
    both = ("y", "z")
    in_specs = (
        P("segment", both, None),
        P(both, None),
        P("segment", None),
        P("segment", both, None, None, None, None),
        P("segment", both, None, None),
        P("segment", both, None),
        P("segment", both, None),
    )
    out_specs = P(None, "segment", both, None)
    return jax.shard_map(
        per_device, mesh=fine, in_specs=in_specs, out_specs=out_specs, check_vma=False
    )
```

```python
import functools

import jax
import jax.numpy as jnp
from jax import lax
from jax.experimental import pallas as pl
from jax.experimental.pallas import tpu as pltpu
from jax.sharding import Mesh, PartitionSpec as P

EPSILON = 1e-06
TILE = 16
VMEM_BYTES = 40 * 2**20
SENT = ((4,), (5, 3), (6, 2, 7, 1, 0))
GIVEN = ((0, 1, 7, 2, 6), (3, 5), (4,))


def shifted(value, axis, by):
    count = lax.axis_size(axis)
    return lax.ppermute(value, axis, [(i, (i + by) % count) for i in range(count)])


def passed_along(shard, axis, by):
    count = lax.axis_size(axis)
    pairs = [(i, i + by) for i in range(count) if 0 <= i + by < count]
    return lax.ppermute(shard, axis, pairs)


def local_call(body, out_shape, operands, flops, scalars=0):
    vmem = pl.BlockSpec(memory_space=pltpu.VMEM)
    smem = pl.BlockSpec(memory_space=pltpu.SMEM)
    moved = sum(v.size * v.dtype.itemsize for v in (*operands, *jax.tree.leaves(out_shape)))
    return pl.pallas_call(
        body,
        out_shape=out_shape,
        in_specs=[smem] * scalars + [vmem] * (len(operands) - scalars),
        out_specs=jax.tree.map(lambda _: vmem, out_shape),
        compiler_params=pltpu.CompilerParams(vmem_limit_bytes=VMEM_BYTES),
        cost_estimate=pl.CostEstimate(flops=flops, bytes_accessed=moved, transcendentals=0),
    )(*operands)


def columns(index, width):
    return pl.ds(pl.multiple_of(index * width, 128), width)


def stream_piece(info, streams, cols):
    if len(streams) == 1:
        return streams[0][:, cols].astype(jnp.float32)
    first = (jnp.zeros((1, 1), jnp.int32) + info[1]) == 0
    return jnp.where(
        first, streams[0][:, cols].astype(jnp.float32), streams[1][:, cols].astype(jnp.float32)
    )


def sending_body(split, groups, n_streams, info, *refs):
    streams, (gain, pick), outs = refs[:n_streams], refs[n_streams : n_streams + 2], refs[n_streams + 2 :]
    width = gain.shape[1] // split
    squares = 0.0
    for piece in range(split):
        values = stream_piece(info, streams, pl.ds(piece * width, width))
        squares = squares + jnp.sum(values * values, axis=1, keepdims=True)
    scale = lax.rsqrt(squares / gain.shape[1] + EPSILON)
    block_rows = pick.shape[0] // groups
    for number, offsets in enumerate(SENT):
        for spot, offset in enumerate(offsets):
            cols = columns(lax.rem(info[0] + offset, split), width)
            normed = (stream_piece(info, streams, cols) * scale * gain[:, cols]).astype(jnp.bfloat16)
            rows = jnp.dot(pick[...], normed, preferred_element_type=jnp.float32)
            rows = rows.astype(jnp.bfloat16)
            for ahead in range(groups):
                outs[number * groups + ahead][spot] = rows[
                    ahead * block_rows : (ahead + 1) * block_rows
                ]


def gathered_body(groups, main, *refs):
    ins, outs = refs[:groups], refs[groups:]
    for spot, out in enumerate(outs):
        rest = ins[0][spot, main:].astype(jnp.float32)
        for ahead in range(groups):
            out[ahead * main : (ahead + 1) * main] = ins[ahead][spot, :main]
            if ahead:
                rest = rest + ins[ahead][spot, main:].astype(jnp.float32)
        out[groups * main :] = rest.astype(jnp.bfloat16)


def spread_body(groups, main, count, *refs):
    ins, outs = refs[:count], refs[count:]
    for spot in range(count):
        for ahead in range(groups):
            outs[ahead][spot, :main] = ins[spot][ahead * main : (ahead + 1) * main]
            outs[ahead][spot, main:] = ins[spot][groups * main :]


def hidden_body(own, low_up, low_down, high_up, high_down, out):
    half = low_up.shape[1]
    for part, (up, down) in enumerate(((low_up, low_down), (high_up, high_down))):
        for block in range(half // 256):
            at = block * 256
            sums = (
                own[:, part * half + at : part * half + at + 256]
                + up[:, at : at + 256].astype(jnp.float32)
                + down[:, at : at + 256].astype(jnp.float32)
            )
            gate, raised = sums[:, :128], sums[:, 128:]
            to = (part * half + at) // 2
            out[:, to : to + 128] = (gate / (1.0 + jnp.exp(-gate)) * raised).astype(jnp.bfloat16)


def combining_body(split, groups, n_streams, n_before, info, *refs):
    streams, (place_back, weight) = refs[:n_streams], refs[n_streams : n_streams + 2]
    before = refs[n_streams + 2 : n_streams + 2 + n_before]
    blocks, out = refs[n_streams + 2 + n_before : -1], refs[-1]
    width = out.shape[-1] // split
    if n_before:
        out[0] = before[0][...]
    for number, offsets in enumerate(GIVEN):
        for spot, offset in enumerate(offsets):
            cols = columns(lax.rem(info[0] + (split - offset), split), width)
            rows = jnp.concatenate(
                [blocks[number * groups + ahead][spot] for ahead in range(groups)], axis=0
            )
            chosen = jnp.dot(place_back[...], rows, preferred_element_type=jnp.float32)
            value = (stream_piece(info, streams, cols) + chosen * weight[...]).astype(jnp.bfloat16)
            if n_before:
                out[1, :, cols] = value
            else:
                out[:, cols] = value


def per_device(tokens, entering, norm_gain, gate_up, down_proj, expert_ids, gate_weights):
    split = lax.axis_size("z")
    groups = lax.axis_size("y")
    row, place = lax.axis_index("y"), lax.axis_index("z")
    info = jnp.stack([place, lax.axis_index("segment")]).astype(jnp.int32)
    tok_rows, model_width = entering.shape
    slot_cap = 9 * tok_rows // (8 * groups)
    main = slot_cap // TILE * TILE
    rest = slot_cap - main
    block_rows = main + groups * rest
    chunk_rows = groups * slot_cap
    piece_width = model_width // split
    hidden_width = down_proj.shape[2]
    half = hidden_width
    far = split // 2
    bf16 = jnp.bfloat16

    flat_ids = expert_ids[0].reshape(tok_rows)
    member = (flat_ids[:, None] == jnp.arange(groups, dtype=jnp.int32)[None, :]).astype(jnp.int32)
    slot_of = jnp.sum((jnp.cumsum(member, axis=0) - 1) * member, axis=1)
    in_block = jnp.where(slot_of < main, slot_of, slot_of + row * rest)
    target = (flat_ids - row + groups) % groups * block_rows + in_block
    all_rows = jnp.arange(groups * block_rows, dtype=jnp.int32)
    pick = (all_rows[:, None] == target[None, :]).astype(bf16)
    place_back = (target[:, None] == all_rows[None, :]).astype(bf16)
    token_weight = gate_weights[0]
    gain = norm_gain
    weights_in = gate_up[0, 0].reshape(piece_width, 2 * hidden_width)
    weights_out = down_proj[0, 0]
    pick_flops = 2 * groups * block_rows * tok_rows * model_width

    def moe_layer(streams, before):
        sent = local_call(
            functools.partial(sending_body, split, groups, len(streams)),
            [
                jax.ShapeDtypeStruct((len(offsets), block_rows, piece_width), bf16)
                for offsets in SENT
                for _ in range(groups)
            ],
            (info, *streams, gain, pick),
            pick_flops,
            1,
        )
        arrived = {}
        for number, offsets in enumerate(SENT):
            blocks = [
                shifted(sent[number * groups + ahead], "y", ahead) if ahead else sent[number * groups]
                for ahead in range(groups)
            ]
            whole = local_call(
                functools.partial(gathered_body, groups, main),
                [jax.ShapeDtypeStruct((chunk_rows, piece_width), bf16) for _ in offsets],
                blocks,
                0,
            )
            for offset, rows in zip(offsets, whole):
                arrived[-offset % split] = shifted(rows, "z", offset) if offset else rows

        def partial_sums(offset):
            return jnp.dot(arrived[offset % split], weights_in, preferred_element_type=jnp.float32)

        opposite = partial_sums(far).astype(bf16)
        low_up, high_down = opposite[:, :half], opposite[:, half:]
        high_up = low_down = None
        for step in range(far - 1, 0, -1):
            low_up = shifted(low_up, "z", 1)
            high_down = shifted(high_down, "z", -1)
            if high_up is not None:
                high_up = shifted(high_up, "z", 1)
                low_down = shifted(low_down, "z", -1)
            ahead, behind = partial_sums(step), partial_sums(-step)
            low_up = (low_up.astype(jnp.float32) + ahead[:, :half]).astype(bf16)
            high_down = (high_down.astype(jnp.float32) + behind[:, half:]).astype(bf16)
            if high_up is None:
                high_up = ahead[:, half:].astype(bf16)
                low_down = behind[:, :half].astype(bf16)
            else:
                high_up = (high_up.astype(jnp.float32) + ahead[:, half:]).astype(bf16)
                low_down = (low_down.astype(jnp.float32) + behind[:, :half]).astype(bf16)
        low_up, high_up = shifted(low_up, "z", 1), shifted(high_up, "z", 1)
        low_down, high_down = shifted(low_down, "z", -1), shifted(high_down, "z", -1)
        hidden = local_call(
            hidden_body,
            jax.ShapeDtypeStruct((chunk_rows, hidden_width), bf16),
            (partial_sums(0), low_up, low_down, high_up, high_down),
            8 * chunk_rows * hidden_width,
        )

        home = {}

        def projected(rows, offset):
            block = jnp.dot(rows, weights_out, preferred_element_type=jnp.float32).astype(bf16)
            home[offset % split] = shifted(block, "z", offset) if offset else block

        from_below = from_above = hidden
        projected(hidden, 0)
        for step in range(1, far):
            from_below = shifted(from_below, "z", 1)
            from_above = shifted(from_above, "z", -1)
            projected(from_below, -step)
            projected(from_above, step)
        left = shifted(from_below[:, : half // 2], "z", 1)
        right = shifted(from_above[:, half // 2 :], "z", -1)
        projected(jnp.concatenate([left, right], axis=1), far)

        returned = []
        for offsets in GIVEN:
            parts = local_call(
                functools.partial(spread_body, groups, main, len(offsets)),
                [
                    jax.ShapeDtypeStruct((len(offsets), block_rows, piece_width), bf16)
                    for _ in range(groups)
                ],
                [home[offset] for offset in offsets],
                0,
            )
            returned += [
                shifted(part, "y", -ahead) if ahead else part for ahead, part in enumerate(parts)
            ]
        return local_call(
            functools.partial(combining_body, split, groups, len(streams), len(before)),
            jax.ShapeDtypeStruct((2,) * len(before) + (tok_rows, model_width), bf16),
            (info, *streams, place_back, token_weight, *before, *returned),
            pick_flops,
            1,
        )

    first_result = moe_layer((tokens[0],), ())
    passed = passed_along(first_result, "segment", 1)
    both_results = moe_layer((entering, passed), (first_result,))
    return both_results[:, None]


def solution(mesh):
    segments, experts = mesh.devices.shape
    split = 8
    fine = Mesh(mesh.devices.reshape(segments, experts // split, split), ("segment", "y", "z"))
    both = ("y", "z")
    in_specs = (
        P("segment", both, None),
        P(both, None),
        P("segment", None),
        P("segment", both, None, None, None, None),
        P("segment", both, None, None),
        P("segment", both, None),
        P("segment", both, None),
    )
    out_specs = P(None, "segment", both, None)
    return jax.shard_map(
        per_device, mesh=fine, in_specs=in_specs, out_specs=out_specs, check_vma=False
    )
```

```python
import functools

import jax
import jax.numpy as jnp
from jax import lax
from jax.experimental import pallas as pl
from jax.experimental.pallas import tpu as pltpu
from jax.sharding import Mesh, PartitionSpec as P

EPSILON = 1e-06
TILE = 16
VMEM_BYTES = 40 * 2**20
BOTH = ("z", "y")


def shifted(value, axis, by):
    count = lax.axis_size(axis)
    return lax.ppermute(value, axis, [(i, (i + by) % count) for i in range(count)])


def passed_along(shard, axis, by):
    count = lax.axis_size(axis)
    pairs = [(i, i + by) for i in range(count) if 0 <= i + by < count]
    return lax.ppermute(shard, axis, pairs)


def exchanged(blocks):
    return lax.all_to_all(blocks, BOTH, split_axis=0, concat_axis=0, tiled=True)


def local_call(body, out_shape, operands, flops, scalars=0):
    vmem = pl.BlockSpec(memory_space=pltpu.VMEM)
    smem = pl.BlockSpec(memory_space=pltpu.SMEM)
    moved = sum(v.size * v.dtype.itemsize for v in (*operands, *jax.tree.leaves(out_shape)))
    return pl.pallas_call(
        body,
        out_shape=out_shape,
        in_specs=[smem] * scalars + [vmem] * (len(operands) - scalars),
        out_specs=jax.tree.map(lambda _: vmem, out_shape),
        compiler_params=pltpu.CompilerParams(vmem_limit_bytes=VMEM_BYTES),
        cost_estimate=pl.CostEstimate(flops=flops, bytes_accessed=moved, transcendentals=0),
    )(*operands)


def stream_piece(info, streams, piece, start, width, total):
    at = piece * total + start
    whole = streams[0][:, at : at + width].astype(jnp.float32)
    if len(streams) == 1:
        return whole
    parts, low = [], 0
    for part in streams[1:]:
        size = part.shape[2]
        if low < start + width and start < low + size:
            left, right = max(start - low, 0), min(start + width - low, size)
            parts.append(part[piece, :, left:right].astype(jnp.float32))
        low += size
    passed = parts[0] if len(parts) == 1 else jnp.concatenate(parts, axis=1)
    first = (jnp.zeros((1, 1), jnp.int32) + info[1]) == 0
    return jnp.where(first, whole, passed)


def sending_body(split, n_streams, info, *refs):
    streams, (gain, pick), out = refs[:n_streams], refs[n_streams : n_streams + 2], refs[-1]
    width = gain.shape[1] // split
    squares = 0.0
    for piece in range(split):
        values = stream_piece(info, streams, piece, 0, width, width)
        squares = squares + jnp.sum(values * values, axis=1, keepdims=True)
    scale = lax.rsqrt(squares / gain.shape[1] + EPSILON)
    groups, block_rows = out.shape[1:3]
    for piece in range(split):
        values = stream_piece(info, streams, piece, 0, width, width)
        normed = values * scale * gain[:, piece * width : (piece + 1) * width]
        rows = jnp.dot(
            pick[...], normed.astype(jnp.bfloat16), preferred_element_type=jnp.float32
        )
        for group in range(groups):
            block = rows[group * block_rows : (group + 1) * block_rows]
            out[piece, group] = block.astype(jnp.bfloat16)


def gathered_body(main, info, arrived, *outs):
    split, groups = arrived.shape[:2]
    for offset, out in enumerate(outs):
        column = lax.rem(info[0] + offset, split)
        blocks = [arrived[column, group].astype(jnp.float32) for group in range(groups)]
        rows = [block[:main] for block in blocks]
        rows += [blocks[i][main:] + blocks[i + 1][main:] for i in range(0, groups, 2)]
        out[...] = jnp.concatenate(rows, axis=0).astype(jnp.bfloat16)


def spread_body(main, info, *refs):
    ins, out = refs[:-1], refs[-1]
    split, groups, block_rows = out.shape[:3]
    rest = block_rows - main
    for offset, rows in enumerate(ins):
        column = lax.rem(info[0] + offset, split)
        values = rows[...].astype(jnp.float32)
        for group in range(groups):
            at = groups * main + group // 2 * rest
            block = [values[group * main : (group + 1) * main], values[at : at + rest]]
            out[column, group] = jnp.concatenate(block, axis=0).astype(jnp.bfloat16)


def hidden_body(own, low_up, low_down, high_up, high_down, low_out, high_out):
    half = low_up.shape[1]
    sides = ((low_up, low_down, low_out), (high_up, high_down, high_out))
    for part, (up, down, out) in enumerate(sides):
        for block in range(half // 256):
            at = block * 256
            sums = (
                own[:, part * half + at : part * half + at + 256]
                + up[:, at : at + 256].astype(jnp.float32)
                + down[:, at : at + 256].astype(jnp.float32)
            )
            gate, raised = sums[:, :128], sums[:, 128:]
            value = gate / (1.0 + jnp.exp(-gate)) * raised
            out[:, block * 128 : (block + 1) * 128] = value.astype(jnp.bfloat16)


def part_body(n_streams, start, info, *refs):
    streams, (place_back, weight, returned, out) = refs[:n_streams], refs[n_streams:]
    split, groups, block_rows, width = returned.shape
    total = streams[0].shape[1] // split
    for piece in range(split):
        rows = jnp.concatenate([returned[piece, group] for group in range(groups)], axis=0)
        chosen = jnp.dot(place_back[...], rows, preferred_element_type=jnp.float32)
        base = stream_piece(info, streams, piece, start, width, total)
        out[piece] = (base + chosen * weight[...]).astype(jnp.bfloat16)


def last_body(n_streams, n_before, parts, info, *refs):
    streams, (place_back, weight) = refs[:n_streams], refs[n_streams : n_streams + 2]
    before = refs[n_streams + 2 : n_streams + 2 + n_before]
    returned, out = refs[n_streams + 2 + n_before : -1], refs[-1]
    split, groups = returned[0].shape[:2]
    total = out.shape[2] // split
    for piece in range(split):
        low = piece * total
        for part in before:
            out[0, :, low : low + part.shape[2]] = part[piece]
            low += part.shape[2]
        for (start, width), blocks in zip(parts, returned):
            rows = jnp.concatenate([blocks[piece, group] for group in range(groups)], axis=0)
            chosen = jnp.dot(place_back[...], rows, preferred_element_type=jnp.float32)
            base = stream_piece(info, streams, piece, start, width, total)
            at = piece * total + start
            out[1, :, at : at + width] = (base + chosen * weight[...]).astype(jnp.bfloat16)


def per_device(tokens, entering, norm_gain, gate_up, down_proj, expert_ids, gate_weights):
    split = lax.axis_size("z")
    groups = lax.axis_size("y")
    row, place = lax.axis_index("y"), lax.axis_index("z")
    info = jnp.stack([place, lax.axis_index("segment")]).astype(jnp.int32)
    tok_rows, model_width = entering.shape
    slot_cap = 9 * tok_rows // (8 * groups)
    main = slot_cap // TILE * TILE
    rest = slot_cap - main
    block_rows = main + 2 * rest
    chunk_rows = groups * slot_cap
    piece_width = model_width // split
    hidden_width = down_proj.shape[2]
    half = hidden_width
    far = split // 2
    bf16, f32 = jnp.bfloat16, jnp.float32

    flat_ids = expert_ids[0].reshape(tok_rows)
    member = (flat_ids[:, None] == jnp.arange(groups, dtype=jnp.int32)[None, :]).astype(jnp.int32)
    slot_of = jnp.sum((jnp.cumsum(member, axis=0) - 1) * member, axis=1)
    in_block = jnp.where(slot_of < main, slot_of, slot_of + row % 2 * rest)
    target = flat_ids * block_rows + in_block
    all_rows = jnp.arange(groups * block_rows, dtype=jnp.int32)
    pick = (all_rows[:, None] == target[None, :]).astype(bf16)
    place_back = (target[:, None] == all_rows[None, :]).astype(bf16)
    token_weight = gate_weights[0]
    weights_in = gate_up[0, 0].reshape(piece_width, 2 * hidden_width)
    weights_out = down_proj[0, 0]
    pick_flops = 2 * groups * block_rows * tok_rows * model_width

    def expert_blocks(streams, parts):
        outgoing = local_call(
            functools.partial(sending_body, split, len(streams)),
            jax.ShapeDtypeStruct((split, groups, block_rows, piece_width), bf16),
            (info, *streams, norm_gain, pick),
            pick_flops,
            1,
        )
        arrived = exchanged(outgoing.reshape(split * groups, block_rows, piece_width))
        arrived = local_call(
            functools.partial(gathered_body, main),
            [jax.ShapeDtypeStruct((chunk_rows, piece_width), bf16)] * split,
            (info, arrived.reshape(split, groups, block_rows, piece_width)),
            0,
            1,
        )

        def partial_sums(offset):
            return jnp.dot(arrived[offset % split], weights_in, preferred_element_type=f32)

        opposite = partial_sums(far).astype(bf16)
        low_up, high_down = opposite[:, :half], opposite[:, half:]
        high_up = low_down = None
        for step in range(far - 1, 0, -1):
            low_up = shifted(low_up, "z", 1)
            high_down = shifted(high_down, "z", -1)
            if high_up is not None:
                high_up = shifted(high_up, "z", 1)
                low_down = shifted(low_down, "z", -1)
            ahead, behind = partial_sums(step), partial_sums(-step)
            low_up = (low_up.astype(f32) + ahead[:, :half]).astype(bf16)
            high_down = (high_down.astype(f32) + behind[:, half:]).astype(bf16)
            if high_up is None:
                high_up = ahead[:, half:].astype(bf16)
                low_down = behind[:, :half].astype(bf16)
            else:
                high_up = (high_up.astype(f32) + ahead[:, half:]).astype(bf16)
                low_down = (low_down.astype(f32) + behind[:, :half]).astype(bf16)
        low_up, high_up = shifted(low_up, "z", 1), shifted(high_up, "z", 1)
        low_down, high_down = shifted(low_down, "z", -1), shifted(high_down, "z", -1)
        low, high = local_call(
            hidden_body,
            [jax.ShapeDtypeStruct((chunk_rows, hidden_width // 2), bf16)] * 2,
            (partial_sums(0), low_up, low_down, high_up, high_down),
            8 * chunk_rows * hidden_width,
        )

        hidden = [None] * split
        hidden[0] = jnp.concatenate([low, high], axis=1)
        low_up = low_down = low
        high_up = high_down = high
        for step in range(1, far):
            low_up, high_up = shifted(low_up, "z", 1), shifted(high_up, "z", 1)
            high_down, low_down = shifted(high_down, "z", -1), shifted(low_down, "z", -1)
            hidden[split - step] = jnp.concatenate([low_up, high_up], axis=1)
            hidden[step] = jnp.concatenate([low_down, high_down], axis=1)
        low_up, high_down = shifted(low_up, "z", 1), shifted(high_down, "z", -1)
        hidden[far] = jnp.concatenate([low_up, high_down], axis=1)
        results = []
        for start, width in parts:
            wanted = weights_out[:, start : start + width]
            blocks = [
                jnp.dot(rows, wanted, preferred_element_type=f32).astype(bf16) for rows in hidden
            ]
            blocks = local_call(
                functools.partial(spread_body, main),
                jax.ShapeDtypeStruct((split, groups, block_rows, width), bf16),
                (info, *blocks),
                0,
                1,
            )
            returned = exchanged(blocks.reshape(split * groups, block_rows, width))
            results.append(returned.reshape(split, groups, block_rows, width))
        return results

    first_streams = (tokens[0],)
    first_parts = ((0, 512), (512, piece_width - 512))
    last_parts = ((0, piece_width),)
    first, passed = [], []
    for (start, width), returned in zip(first_parts, expert_blocks(first_streams, first_parts)):
        first.append(
            local_call(
                functools.partial(part_body, len(first_streams), start),
                jax.ShapeDtypeStruct((split, tok_rows, width), bf16),
                (info, *first_streams, place_back, token_weight, returned),
                pick_flops,
                1,
            )
        )
        passed.append(passed_along(first[-1], "segment", 1))
    second_streams = (entering, *passed)
    returned = expert_blocks(second_streams, last_parts)
    results = local_call(
        functools.partial(last_body, len(second_streams), len(first), last_parts),
        jax.ShapeDtypeStruct((2, tok_rows, model_width), bf16),
        (info, *second_streams, place_back, token_weight, *first, *returned),
        pick_flops,
        1,
    )
    return results[:, None]


def solution(mesh):
    segments, experts = mesh.devices.shape
    split = 8
    fine = Mesh(mesh.devices.reshape(segments, experts // split, split), ("segment", "y", "z"))
    both = ("y", "z")
    in_specs = (
        P("segment", both, None),
        P(both, None),
        P("segment", None),
        P("segment", both, None, None, None, None),
        P("segment", both, None, None),
        P("segment", both, None),
        P("segment", both, None),
    )
    out_specs = P(None, "segment", both, None)
    return jax.shard_map(
        per_device, mesh=fine, in_specs=in_specs, out_specs=out_specs, check_vma=False
    )
```

```python
import functools

import jax
import jax.numpy as jnp
from jax import lax
from jax.experimental import pallas as pl
from jax.experimental.pallas import tpu as pltpu
from jax.sharding import Mesh, PartitionSpec as P

EPSILON = 1e-06
TILE = 16
VMEM_BYTES = 40 * 2**20
BOTH = ("z", "y")
GIVEN = ((0, 1, 7), (2, 6), (3, 5), (4,))
PARTS = (GIVEN[:2], GIVEN[2:])


def shifted(value, axis, by):
    count = lax.axis_size(axis)
    return lax.ppermute(value, axis, [(i, (i + by) % count) for i in range(count)])


def passed_along(shard, axis, by):
    count = lax.axis_size(axis)
    pairs = [(i, i + by) for i in range(count) if 0 <= i + by < count]
    return lax.ppermute(shard, axis, pairs)


def exchanged(blocks):
    return lax.all_to_all(blocks, BOTH, split_axis=0, concat_axis=0, tiled=True)


def local_call(body, out_shape, operands, flops, scalars=0):
    vmem = pl.BlockSpec(memory_space=pltpu.VMEM)
    smem = pl.BlockSpec(memory_space=pltpu.SMEM)
    moved = sum(v.size * v.dtype.itemsize for v in (*operands, *jax.tree.leaves(out_shape)))
    return pl.pallas_call(
        body,
        out_shape=out_shape,
        in_specs=[smem] * scalars + [vmem] * (len(operands) - scalars),
        out_specs=jax.tree.map(lambda _: vmem, out_shape),
        compiler_params=pltpu.CompilerParams(vmem_limit_bytes=VMEM_BYTES),
        cost_estimate=pl.CostEstimate(flops=flops, bytes_accessed=moved, transcendentals=0),
    )(*operands)


def columns(index, width):
    return pl.ds(pl.multiple_of(index * width, 128), width)


def piece_of(info, offset, split):
    return lax.rem(info[0] + (split - offset), split)


def stream_piece(info, streams, offset, split):
    width = streams[0].shape[1] // split
    cols = columns(piece_of(info, offset, split), width)
    whole = streams[0][:, cols].astype(jnp.float32)
    if len(streams) == 1:
        return whole
    for part, groups in zip(streams[1:], PARTS):
        offsets = [number for group in groups for number in group]
        if offset in offsets:
            passed = part[offsets.index(offset)].astype(jnp.float32)
    first = (jnp.zeros((1, 1), jnp.int32) + info[1]) == 0
    return jnp.where(first, whole, passed)


def sending_body(split, n_streams, info, *refs):
    streams, (gain, pick), out = refs[:n_streams], refs[n_streams : n_streams + 2], refs[-1]
    width = gain.shape[1] // split
    squares = 0.0
    for offset in range(split):
        values = stream_piece(info, streams, offset, split)
        squares = squares + jnp.sum(values * values, axis=1, keepdims=True)
    scale = lax.rsqrt(squares / gain.shape[1] + EPSILON)
    groups, block_rows = out.shape[1:3]
    for offset in range(split):
        piece = piece_of(info, offset, split)
        values = stream_piece(info, streams, offset, split)
        normed = values * scale * gain[:, columns(piece, width)]
        rows = jnp.dot(
            pick[...], normed.astype(jnp.bfloat16), preferred_element_type=jnp.float32
        )
        for group in range(groups):
            block = rows[group * block_rows : (group + 1) * block_rows]
            out[piece, group] = block.astype(jnp.bfloat16)


def gathered_body(main, info, arrived, *outs):
    split, groups = arrived.shape[:2]
    for offset, out in enumerate(outs):
        column = lax.rem(info[0] + offset, split)
        blocks = [arrived[column, group].astype(jnp.float32) for group in range(groups)]
        rows = [block[:main] for block in blocks]
        rows += [blocks[i][main:] + blocks[i + 1][main:] for i in range(0, groups, 2)]
        out[...] = jnp.concatenate(rows, axis=0).astype(jnp.bfloat16)


def spread_body(groups, main, count, info, *refs):
    ins, outs = refs[:count], refs[count:]
    for spot in range(count):
        for ahead in range(groups):
            row = lax.rem(info[2] + (groups - ahead), groups)
            outs[ahead][spot, :main] = ins[spot][pl.ds(pl.multiple_of(row * main, TILE), main)]
            outs[ahead][spot, main:] = ins[spot][groups * main :]


def hidden_body(own, low_up, low_down, high_up, high_down, low_out, high_out):
    half = low_up.shape[1]
    sides = ((low_up, low_down, low_out), (high_up, high_down, high_out))
    for part, (up, down, out) in enumerate(sides):
        for block in range(half // 256):
            at = block * 256
            sums = (
                own[:, part * half + at : part * half + at + 256]
                + up[:, at : at + 256].astype(jnp.float32)
                + down[:, at : at + 256].astype(jnp.float32)
            )
            gate, raised = sums[:, :128], sums[:, 128:]
            value = gate / (1.0 + jnp.exp(-gate)) * raised
            out[:, block * 128 : (block + 1) * 128] = value.astype(jnp.bfloat16)


def combined(info, streams, place_back, weight, blocks, spot, offset, split):
    rows = jnp.concatenate([block[spot] for block in blocks], axis=0)
    chosen = jnp.dot(place_back[...], rows, preferred_element_type=jnp.float32)
    base = stream_piece(info, streams, offset, split)
    return (base + chosen * weight[...]).astype(jnp.bfloat16)


def part_body(split, groups, given, info, stream, place_back, weight, *refs):
    blocks, out = refs[:-1], refs[-1]
    at = 0
    for number, offsets in enumerate(given):
        mine = blocks[number * groups : (number + 1) * groups]
        for spot, offset in enumerate(offsets):
            out[at] = combined(info, (stream,), place_back, weight, mine, spot, offset, split)
            at += 1


def last_body(split, groups, info, *refs):
    streams, (place_back, weight) = refs[:3], refs[3:5]
    before, blocks, out = refs[5:7], refs[7:-1], refs[-1]
    width = out.shape[2] // split
    number = 0
    for part, given in zip(before, PARTS):
        at = 0
        for offsets in given:
            mine = blocks[number * groups : (number + 1) * groups]
            for spot, offset in enumerate(offsets):
                cols = columns(piece_of(info, offset, split), width)
                out[0, :, cols] = part[at]
                out[1, :, cols] = combined(
                    info, streams, place_back, weight, mine, spot, offset, split
                )
                at += 1
            number += 1


def per_device(tokens, entering, norm_gain, gate_up, down_proj, expert_ids, gate_weights):
    split = lax.axis_size("z")
    groups = lax.axis_size("y")
    row, place = lax.axis_index("y"), lax.axis_index("z")
    info = jnp.stack([place, lax.axis_index("segment"), row]).astype(jnp.int32)
    tok_rows, model_width = entering.shape
    slot_cap = 9 * tok_rows // (8 * groups)
    main = slot_cap // TILE * TILE
    rest = slot_cap - main
    block_rows = main + 2 * rest
    chunk_rows = groups * slot_cap
    piece_width = model_width // split
    hidden_width = down_proj.shape[2]
    half = hidden_width
    far = split // 2
    bf16, f32 = jnp.bfloat16, jnp.float32

    flat_ids = expert_ids[0].reshape(tok_rows)
    member = (flat_ids[:, None] == jnp.arange(groups, dtype=jnp.int32)[None, :]).astype(jnp.int32)
    slot_of = jnp.sum((jnp.cumsum(member, axis=0) - 1) * member, axis=1)
    in_block = jnp.where(slot_of < main, slot_of, slot_of + row % 2 * rest)
    target = flat_ids * block_rows + in_block
    all_rows = jnp.arange(groups * block_rows, dtype=jnp.int32)
    pick = (all_rows[:, None] == target[None, :]).astype(bf16)
    back_rows = main + groups * rest
    in_block = jnp.where(slot_of < main, slot_of, slot_of + row * rest)
    origin = (flat_ids - row + groups) % groups * back_rows + in_block
    origin_rows = jnp.arange(groups * back_rows, dtype=jnp.int32)
    place_back = (origin[:, None] == origin_rows[None, :]).astype(bf16)
    token_weight = gate_weights[0]
    weights_in = gate_up[0, 0].reshape(piece_width, 2 * hidden_width)
    weights_out = down_proj[0, 0]
    pick_flops = 2 * groups * block_rows * tok_rows * model_width

    def expert_blocks(streams):
        outgoing = local_call(
            functools.partial(sending_body, split, len(streams)),
            jax.ShapeDtypeStruct((split, groups, block_rows, piece_width), bf16),
            (info, *streams, norm_gain, pick),
            pick_flops,
            1,
        )
        arrived = exchanged(outgoing.reshape(split * groups, block_rows, piece_width))
        arrived = local_call(
            functools.partial(gathered_body, main),
            [jax.ShapeDtypeStruct((chunk_rows, piece_width), bf16)] * split,
            (info, arrived.reshape(split, groups, block_rows, piece_width)),
            0,
            1,
        )

        def partial_sums(offset):
            return jnp.dot(arrived[offset % split], weights_in, preferred_element_type=f32)

        opposite = partial_sums(far).astype(bf16)
        low_up, high_down = opposite[:, :half], opposite[:, half:]
        high_up = low_down = None
        for step in range(far - 1, 0, -1):
            low_up = shifted(low_up, "z", 1)
            high_down = shifted(high_down, "z", -1)
            if high_up is not None:
                high_up = shifted(high_up, "z", 1)
                low_down = shifted(low_down, "z", -1)
            ahead, behind = partial_sums(step), partial_sums(-step)
            low_up = (low_up.astype(f32) + ahead[:, :half]).astype(bf16)
            high_down = (high_down.astype(f32) + behind[:, half:]).astype(bf16)
            if high_up is None:
                high_up = ahead[:, half:].astype(bf16)
                low_down = behind[:, :half].astype(bf16)
            else:
                high_up = (high_up.astype(f32) + ahead[:, half:]).astype(bf16)
                low_down = (low_down.astype(f32) + behind[:, :half]).astype(bf16)
        low_up, high_up = shifted(low_up, "z", 1), shifted(high_up, "z", 1)
        low_down, high_down = shifted(low_down, "z", -1), shifted(high_down, "z", -1)
        low, high = local_call(
            hidden_body,
            [jax.ShapeDtypeStruct((chunk_rows, hidden_width // 2), bf16)] * 2,
            (partial_sums(0), low_up, low_down, high_up, high_down),
            8 * chunk_rows * hidden_width,
        )

        home = [None] * split

        def projected(rows, offset):
            block = jnp.dot(rows, weights_out, preferred_element_type=f32).astype(bf16)
            home[offset] = shifted(block, "z", offset) if offset else block
            return block

        projected(jnp.concatenate([low, high], axis=1), 0)
        low_up = low_down = low
        high_up = high_down = high
        for step in range(1, far):
            low_up, high_up = shifted(low_up, "z", 1), shifted(high_up, "z", 1)
            high_down, low_down = shifted(high_down, "z", -1), shifted(low_down, "z", -1)
            projected(jnp.concatenate([low_up, high_up], axis=1), split - step)
            latest = projected(jnp.concatenate([low_down, high_down], axis=1), step)
        low_up, high_down = shifted(low_up, "z", 1), shifted(high_down, "z", -1)
        farthest = projected(jnp.concatenate([low_up, high_down], axis=1), far)
        returned = []
        for offsets in GIVEN:
            blocks = [home[offset] for offset in offsets]
            if far not in offsets:
                ahead_of = latest if 0 in offsets else farthest
                blocks = lax.optimization_barrier((*blocks, ahead_of))[:-1]
            spread = local_call(
                functools.partial(spread_body, groups, main, len(offsets)),
                [jax.ShapeDtypeStruct((len(offsets), back_rows, piece_width), bf16)] * groups,
                (info, *blocks),
                0,
                1,
            )
            returned.append(
                [shifted(part, "y", -ahead) if ahead else part for ahead, part in enumerate(spread)]
            )
        return returned, home[far - 1 : far + 2]

    returned, last_home = expert_blocks((tokens[0],))
    first, passed, number = [], [], 0
    for given in PARTS:
        blocks = sum(returned[number : number + len(given)], [])
        number += len(given)
        if number < len(GIVEN):
            blocks = lax.optimization_barrier((*blocks, *last_home))[: len(blocks)]
        first.append(
            local_call(
                functools.partial(part_body, split, groups, given),
                jax.ShapeDtypeStruct((sum(map(len, given)), tok_rows, piece_width), bf16),
                (info, tokens[0], place_back, token_weight, *blocks),
                pick_flops,
                1,
            )
        )
        passed.append(passed_along(first[-1], "segment", 1))
    second_streams = (entering, *passed)
    returned, _ = expert_blocks(second_streams)
    results = local_call(
        functools.partial(last_body, split, groups),
        jax.ShapeDtypeStruct((2, tok_rows, model_width), bf16),
        (info, *second_streams, place_back, token_weight, *first, *sum(returned, [])),
        pick_flops,
        1,
    )
    return results[:, None]


def solution(mesh):
    segments, experts = mesh.devices.shape
    split = 8
    fine = Mesh(mesh.devices.reshape(segments, experts // split, split), ("segment", "y", "z"))
    both = ("y", "z")
    in_specs = (
        P("segment", both, None),
        P(both, None),
        P("segment", None),
        P("segment", both, None, None, None, None),
        P("segment", both, None, None),
        P("segment", both, None),
        P("segment", both, None),
    )
    out_specs = P(None, "segment", both, None)
    return jax.shard_map(
        per_device, mesh=fine, in_specs=in_specs, out_specs=out_specs, check_vma=False
    )
```

```python
import functools

import jax
import jax.numpy as jnp
from jax import lax
from jax.experimental import pallas as pl
from jax.experimental.pallas import tpu as pltpu
from jax.sharding import Mesh, PartitionSpec as P

EPSILON = 1e-06
TILE = 16
LANES = 128
VMEM_BYTES = 40 * 2**20
BOTH = ("z", "y")


def shifted(value, axis, by):
    count = lax.axis_size(axis)
    return lax.ppermute(value, axis, [(i, (i + by) % count) for i in range(count)])


def passed_along(shard, axis, by):
    count = lax.axis_size(axis)
    pairs = [(i, i + by) for i in range(count) if 0 <= i + by < count]
    return lax.ppermute(shard, axis, pairs)


def packed_rows(main, rest, width):
    tiles = width // LANES
    return tiles * main + (tiles + 1) // 2 * 2 * rest


def lanes(tile):
    return slice(tile * LANES, (tile + 1) * LANES)


def upper_half(rest):
    return lax.broadcasted_iota(jnp.int32, (2 * rest, LANES), 0) // rest


def exchanged(blocks):
    return lax.all_to_all(blocks, BOTH, split_axis=0, concat_axis=0, tiled=True)


def local_call(body, out_shape, operands, flops, scalars=0):
    vmem = pl.BlockSpec(memory_space=pltpu.VMEM)
    smem = pl.BlockSpec(memory_space=pltpu.SMEM)
    moved = sum(v.size * v.dtype.itemsize for v in (*operands, *jax.tree.leaves(out_shape)))
    return pl.pallas_call(
        body,
        out_shape=out_shape,
        in_specs=[smem] * scalars + [vmem] * (len(operands) - scalars),
        out_specs=jax.tree.map(lambda _: vmem, out_shape),
        compiler_params=pltpu.CompilerParams(vmem_limit_bytes=VMEM_BYTES),
        cost_estimate=pl.CostEstimate(flops=flops, bytes_accessed=moved, transcendentals=0),
    )(*operands)


def stream_piece(info, streams, piece, start, width, total):
    at = piece * total + start
    whole = streams[0][:, at : at + width].astype(jnp.float32)
    if len(streams) == 1:
        return whole
    parts, low = [], 0
    for part in streams[1:]:
        size = part.shape[2]
        if low < start + width and start < low + size:
            left, right = max(start - low, 0), min(start + width - low, size)
            parts.append(part[piece, :, left:right].astype(jnp.float32))
        low += size
    passed = parts[0] if len(parts) == 1 else jnp.concatenate(parts, axis=1)
    first = (jnp.zeros((1, 1), jnp.int32) + info[1]) == 0
    return jnp.where(first, whole, passed)


def sending_body(split, main, rest, n_streams, info, *refs):
    streams, (gain, pick), out = refs[:n_streams], refs[n_streams : n_streams + 2], refs[-1]
    width = gain.shape[1] // split
    tiles = width // LANES
    groups = out.shape[1]
    block_rows = main + 2 * rest
    own_half = upper_half(rest) == lax.rem(info[2], 2)
    squares = 0.0
    for piece in range(split):
        values = stream_piece(info, streams, piece, 0, width, width)
        squares = squares + jnp.sum(values * values, axis=1, keepdims=True)
    scale = lax.rsqrt(squares / gain.shape[1] + EPSILON)
    for piece in range(split):
        values = stream_piece(info, streams, piece, 0, width, width)
        normed = values * scale * gain[:, piece * width : (piece + 1) * width]
        rows = jnp.dot(
            pick[...], normed.astype(jnp.bfloat16), preferred_element_type=jnp.float32
        )
        for group in range(groups):
            block = rows[group * block_rows : (group + 1) * block_rows]
            for tile in range(tiles):
                value = block[:main, lanes(tile)].astype(jnp.bfloat16)
                out[piece, group, tile * main : (tile + 1) * main] = value
            last = []
            for tile in range(0, tiles, 2):
                here = block[main:, lanes(tile)]
                after = block[main:, lanes(min(tile + 1, tiles - 1))]
                last.append(jnp.where(own_half, here, after))
            value = jnp.concatenate(last, axis=0).astype(jnp.bfloat16)
            out[piece, group, tiles * main :] = value


def gathered_body(main, rest, info, arrived, *outs):
    split, groups = arrived.shape[:2]
    tiles = outs[0].shape[1] // LANES
    lower = upper_half(rest) == 0
    for offset, out in enumerate(outs):
        column = lax.rem(info[0] + offset, split)
        ends = []
        for group in range(groups):
            for tile in range(tiles):
                value = arrived[column, group, tile * main : (tile + 1) * main]
                out[group * main : (group + 1) * main, lanes(tile)] = value
            ends.append(arrived[column, group, tiles * main :].astype(jnp.float32))
        for tile in range(tiles):
            at = slice(tile // 2 * 2 * rest, (tile // 2 + 1) * 2 * rest)
            pairs = []
            for group in range(0, groups, 2):
                even, odd = ends[group][at], ends[group + 1][at]
                if tile % 2 == 0:
                    pairs.append(jnp.where(lower, even, odd))
                else:
                    pairs.append(pltpu.roll(jnp.where(lower, odd, even), rest, 0))
            value = jnp.concatenate(pairs, axis=0).astype(jnp.bfloat16)
            out[groups * main :, lanes(tile)] = value


def spread_body(main, rest, info, *refs):
    ins, out = refs[:-1], refs[-1]
    split, groups = out.shape[:2]
    tiles = ins[0].shape[1] // LANES
    lower = upper_half(rest) == 0
    for offset, rows in enumerate(ins):
        column = lax.rem(info[0] + offset, split)
        ends = rows[groups * main :].astype(jnp.float32)
        for group in range(groups):
            for tile in range(tiles):
                value = rows[group * main : (group + 1) * main, lanes(tile)]
                out[column, group, tile * main : (tile + 1) * main] = value
            mine = ends[group // 2 * 2 * rest : (group // 2 + 1) * 2 * rest]
            last = []
            for tile in range(0, tiles, 2):
                here = mine[:, lanes(tile)]
                after = pltpu.roll(mine[:, lanes(min(tile + 1, tiles - 1))], rest, 0)
                low, high = (here, after) if group % 2 == 0 else (after, here)
                last.append(jnp.where(lower, low, high))
            value = jnp.concatenate(last, axis=0).astype(jnp.bfloat16)
            out[column, group, tiles * main :] = value


def hidden_body(own, low_up, low_down, high_up, high_down, low_out, high_out):
    half = low_up.shape[1]
    sides = ((low_up, low_down, low_out), (high_up, high_down, high_out))
    for part, (up, down, out) in enumerate(sides):
        for block in range(half // 256):
            at = block * 256
            sums = (
                own[:, part * half + at : part * half + at + 256]
                + up[:, at : at + 256].astype(jnp.float32)
                + down[:, at : at + 256].astype(jnp.float32)
            )
            gate, raised = sums[:, :128], sums[:, 128:]
            value = gate / (1.0 + jnp.exp(-gate)) * raised
            out[:, block * 128 : (block + 1) * 128] = value.astype(jnp.bfloat16)


def chosen_rows(main, place_main, place_rest, returned, piece):
    groups = returned.shape[1]
    tiles = place_rest.shape[0] // LANES
    whole = [
        jnp.concatenate(
            [returned[piece, group, tile * main : (tile + 1) * main] for group in range(groups)],
            axis=0,
        )
        for tile in range(tiles)
    ]
    chosen = jnp.dot(
        place_main[...], jnp.concatenate(whole, axis=1), preferred_element_type=jnp.float32
    )
    ends = [returned[piece, group, tiles * main :] for group in range(groups)]
    others = jnp.dot(
        place_rest[...], jnp.concatenate(ends, axis=0), preferred_element_type=jnp.float32
    )
    return chosen + jnp.concatenate([others[lanes(tile)] for tile in range(tiles)], axis=1)


def part_body(split, main, n_streams, start, info, *refs):
    streams = refs[:n_streams]
    place_main, weight, place_rest, returned, out = refs[n_streams:]
    width = out.shape[2]
    total = streams[0].shape[1] // split
    for piece in range(split):
        chosen = chosen_rows(main, place_main, place_rest, returned, piece)
        base = stream_piece(info, streams, piece, start, width, total)
        out[piece] = (base + chosen * weight[...]).astype(jnp.bfloat16)


def last_body(split, main, n_streams, n_before, info, *refs):
    streams, before = refs[:n_streams], refs[n_streams : n_streams + n_before]
    place_main, weight, place_rest, returned, out = refs[n_streams + n_before :]
    total = out.shape[2] // split
    for piece in range(split):
        low = piece * total
        for part in before:
            out[0, :, low : low + part.shape[2]] = part[piece]
            low += part.shape[2]
        chosen = chosen_rows(main, place_main, place_rest, returned, piece)
        base = stream_piece(info, streams, piece, 0, total, total)
        value = (base + chosen * weight[...]).astype(jnp.bfloat16)
        out[1, :, piece * total : (piece + 1) * total] = value


def per_device(tokens, entering, norm_gain, gate_up, down_proj, expert_ids, gate_weights):
    split = lax.axis_size("z")
    groups = lax.axis_size("y")
    row, place = lax.axis_index("y"), lax.axis_index("z")
    info = jnp.stack([place, lax.axis_index("segment"), row]).astype(jnp.int32)
    tok_rows, model_width = entering.shape
    slot_cap = 9 * tok_rows // (8 * groups)
    main = slot_cap // TILE * TILE
    rest = slot_cap - main
    block_rows = main + 2 * rest
    chunk_rows = groups * slot_cap
    piece_width = model_width // split
    hidden_width = down_proj.shape[2]
    half = hidden_width
    far = split // 2
    bf16, f32 = jnp.bfloat16, jnp.float32

    flat_ids = expert_ids[0].reshape(tok_rows)
    member = (flat_ids[:, None] == jnp.arange(groups, dtype=jnp.int32)[None, :]).astype(jnp.int32)
    slot_of = jnp.sum((jnp.cumsum(member, axis=0) - 1) * member, axis=1)
    block_places = jnp.arange(groups * block_rows, dtype=jnp.int32)
    places = flat_ids * block_rows + slot_of
    again = jnp.where(slot_of < main, places, places + rest)
    pick = (block_places[:, None] == places[None, :]) | (block_places[:, None] == again[None, :])
    pick = pick.astype(bf16)
    main_rows = jnp.arange(groups * main, dtype=jnp.int32)
    origin = jnp.where(slot_of < main, flat_ids * main + slot_of, -1)
    place_main = (origin[:, None] == main_rows[None, :]).astype(bf16)

    def place_rest(width):
        tiles = width // LANES
        end_rows = (tiles + 1) // 2 * 2 * rest
        tile = jnp.arange(tiles, dtype=jnp.int32)[:, None]
        at = flat_ids * end_rows + slot_of - main
        at = at[None, :] + tile // 2 * 2 * rest + (tile + row) % 2 * rest
        at = jnp.where(slot_of[None, :] < main, -1, at).reshape(tiles * tok_rows)
        rows = jnp.arange(groups * end_rows, dtype=jnp.int32)
        return (at[:, None] == rows[None, :]).astype(bf16)

    token_weight = gate_weights[0]
    weights_in = gate_up[0, 0].reshape(piece_width, 2 * hidden_width)
    weights_out = down_proj[0, 0]
    pick_flops = 2 * groups * block_rows * tok_rows * model_width

    def expert_blocks(streams, parts):
        sent_rows = packed_rows(main, rest, piece_width)
        outgoing = local_call(
            functools.partial(sending_body, split, main, rest, len(streams)),
            jax.ShapeDtypeStruct((split, groups, sent_rows, LANES), bf16),
            (info, *streams, norm_gain, pick),
            pick_flops,
            1,
        )
        arrived = exchanged(outgoing.reshape(split * groups, sent_rows, LANES))
        arrived = local_call(
            functools.partial(gathered_body, main, rest),
            [jax.ShapeDtypeStruct((chunk_rows, piece_width), bf16)] * split,
            (info, arrived.reshape(split, groups, sent_rows, LANES)),
            0,
            1,
        )

        def partial_sums(offset):
            return jnp.dot(arrived[offset % split], weights_in, preferred_element_type=f32)

        opposite = partial_sums(far).astype(bf16)
        low_up, high_down = opposite[:, :half], opposite[:, half:]
        high_up = low_down = None
        for step in range(far - 1, 0, -1):
            low_up = shifted(low_up, "z", 1)
            high_down = shifted(high_down, "z", -1)
            if high_up is not None:
                high_up = shifted(high_up, "z", 1)
                low_down = shifted(low_down, "z", -1)
            ahead, behind = partial_sums(step), partial_sums(-step)
            low_up = (low_up.astype(f32) + ahead[:, :half]).astype(bf16)
            high_down = (high_down.astype(f32) + behind[:, half:]).astype(bf16)
            if high_up is None:
                high_up = ahead[:, half:].astype(bf16)
                low_down = behind[:, :half].astype(bf16)
            else:
                high_up = (high_up.astype(f32) + ahead[:, half:]).astype(bf16)
                low_down = (low_down.astype(f32) + behind[:, :half]).astype(bf16)
        low_up, high_up = shifted(low_up, "z", 1), shifted(high_up, "z", 1)
        low_down, high_down = shifted(low_down, "z", -1), shifted(high_down, "z", -1)
        low, high = local_call(
            hidden_body,
            [jax.ShapeDtypeStruct((chunk_rows, hidden_width // 2), bf16)] * 2,
            (partial_sums(0), low_up, low_down, high_up, high_down),
            8 * chunk_rows * hidden_width,
        )

        hidden = [None] * split
        hidden[0] = jnp.concatenate([low, high], axis=1)
        low_up = low_down = low
        high_up = high_down = high
        for step in range(1, far):
            low_up, high_up = shifted(low_up, "z", 1), shifted(high_up, "z", 1)
            high_down, low_down = shifted(high_down, "z", -1), shifted(low_down, "z", -1)
            hidden[split - step] = jnp.concatenate([low_up, high_up], axis=1)
            hidden[step] = jnp.concatenate([low_down, high_down], axis=1)
        low_up, high_down = shifted(low_up, "z", 1), shifted(high_down, "z", -1)
        hidden[far] = jnp.concatenate([low_up, high_down], axis=1)
        results = []
        for start, width in parts:
            wanted = weights_out[:, start : start + width]
            blocks = [
                jnp.dot(rows, wanted, preferred_element_type=f32).astype(bf16) for rows in hidden
            ]
            given_rows = packed_rows(main, rest, width)
            blocks = local_call(
                functools.partial(spread_body, main, rest),
                jax.ShapeDtypeStruct((split, groups, given_rows, LANES), bf16),
                (info, *blocks),
                0,
                1,
            )
            returned = exchanged(blocks.reshape(split * groups, given_rows, LANES))
            results.append(returned.reshape(split, groups, given_rows, LANES))
        return results

    first_streams = (tokens[0],)
    first_parts = ((0, 512), (512, piece_width - 512))
    last_parts = ((0, piece_width),)
    first, passed = [], []
    for (start, width), returned in zip(first_parts, expert_blocks(first_streams, first_parts)):
        first.append(
            local_call(
                functools.partial(part_body, split, main, len(first_streams), start),
                jax.ShapeDtypeStruct((split, tok_rows, width), bf16),
                (info, *first_streams, place_main, token_weight, place_rest(width), returned),
                pick_flops,
                1,
            )
        )
        passed.append(passed_along(first[-1], "segment", 1))
    second_streams = (entering, *passed)
    (returned,) = expert_blocks(second_streams, last_parts)
    results = local_call(
        functools.partial(last_body, split, main, len(second_streams), len(first)),
        jax.ShapeDtypeStruct((2, tok_rows, model_width), bf16),
        (
            info,
            *second_streams,
            *first,
            place_main,
            token_weight,
            place_rest(piece_width),
            returned,
        ),
        pick_flops,
        1,
    )
    return results[:, None]


def solution(mesh):
    segments, experts = mesh.devices.shape
    split = 8
    fine = Mesh(mesh.devices.reshape(segments, experts // split, split), ("segment", "y", "z"))
    both = ("y", "z")
    in_specs = (
        P("segment", both, None),
        P(both, None),
        P("segment", None),
        P("segment", both, None, None, None, None),
        P("segment", both, None, None),
        P("segment", both, None),
        P("segment", both, None),
    )
    out_specs = P(None, "segment", both, None)
    return jax.shard_map(
        per_device, mesh=fine, in_specs=in_specs, out_specs=out_specs, check_vma=False
    )
```

```python
import functools

import jax
import jax.numpy as jnp
from jax import lax
from jax.experimental import pallas as pl
from jax.experimental.pallas import tpu as pltpu
from jax.sharding import Mesh, PartitionSpec as P

EPSILON = 1e-06
TILE = 16
LANES = 128
VMEM_BYTES = 40 * 2**20
BOTH = ("z", "y")


def shifted(value, axis, by):
    count = lax.axis_size(axis)
    return lax.ppermute(value, axis, [(i, (i + by) % count) for i in range(count)])


def passed_along(shard, axis, by):
    count = lax.axis_size(axis)
    pairs = [(i, i + by) for i in range(count) if 0 <= i + by < count]
    return lax.ppermute(shard, axis, pairs)


def packed_rows(main, rest, width):
    tiles = width // LANES
    return tiles * main + (tiles + 1) // 2 * 2 * rest


def lanes(tile):
    return slice(tile * LANES, (tile + 1) * LANES)


def upper_half(rest):
    return lax.broadcasted_iota(jnp.int32, (2 * rest, LANES), 0) // rest


def exchanged(blocks):
    return lax.all_to_all(blocks, BOTH, split_axis=0, concat_axis=0, tiled=True)


def local_call(body, out_shape, operands, flops, scalars=0):
    vmem = pl.BlockSpec(memory_space=pltpu.VMEM)
    smem = pl.BlockSpec(memory_space=pltpu.SMEM)
    moved = sum(v.size * v.dtype.itemsize for v in (*operands, *jax.tree.leaves(out_shape)))
    return pl.pallas_call(
        body,
        out_shape=out_shape,
        in_specs=[smem] * scalars + [vmem] * (len(operands) - scalars),
        out_specs=jax.tree.map(lambda _: vmem, out_shape),
        compiler_params=pltpu.CompilerParams(vmem_limit_bytes=VMEM_BYTES),
        cost_estimate=pl.CostEstimate(flops=flops, bytes_accessed=moved, transcendentals=0),
    )(*operands)


def stream_piece(info, streams, piece, start, width, total):
    at = piece * total + start
    whole = streams[0][:, at : at + width].astype(jnp.float32)
    if len(streams) == 1:
        return whole
    parts, low = [], 0
    for part in streams[1:]:
        size = part.shape[2]
        if low < start + width and start < low + size:
            left, right = max(start - low, 0), min(start + width - low, size)
            parts.append(part[piece, :, left:right].astype(jnp.float32))
        low += size
    passed = parts[0] if len(parts) == 1 else jnp.concatenate(parts, axis=1)
    first = (jnp.zeros((1, 1), jnp.int32) + info[1]) == 0
    return jnp.where(first, whole, passed)


def sending_body(split, main, rest, n_streams, info, *refs):
    streams, (gain, pick), out = refs[:n_streams], refs[n_streams : n_streams + 2], refs[-1]
    width = gain.shape[1] // split
    tiles = width // LANES
    groups = out.shape[1]
    block_rows = main + 2 * rest
    own_half = upper_half(rest) == lax.rem(info[2], 2)
    squares = 0.0
    for piece in range(split):
        values = stream_piece(info, streams, piece, 0, width, width)
        squares = squares + jnp.sum(values * values, axis=1, keepdims=True)
    scale = lax.rsqrt(squares / gain.shape[1] + EPSILON)
    for piece in range(split):
        values = stream_piece(info, streams, piece, 0, width, width)
        normed = values * scale * gain[:, piece * width : (piece + 1) * width]
        rows = jnp.dot(
            pick[...], normed.astype(jnp.bfloat16), preferred_element_type=jnp.float32
        )
        for group in range(groups):
            block = rows[group * block_rows : (group + 1) * block_rows]
            for tile in range(tiles):
                value = block[:main, lanes(tile)].astype(jnp.bfloat16)
                out[piece, group, tile * main : (tile + 1) * main] = value
            last = []
            for tile in range(0, tiles, 2):
                here = block[main:, lanes(tile)]
                after = block[main:, lanes(min(tile + 1, tiles - 1))]
                last.append(jnp.where(own_half, here, after))
            value = jnp.concatenate(last, axis=0).astype(jnp.bfloat16)
            out[piece, group, tiles * main :] = value


def gathered_body(main, rest, info, arrived, *outs):
    split, groups = arrived.shape[:2]
    tiles = outs[0].shape[1] // LANES
    lower = upper_half(rest) == 0
    for offset, out in enumerate(outs):
        column = lax.rem(info[0] + offset, split)
        ends = []
        for group in range(groups):
            for tile in range(tiles):
                value = arrived[column, group, tile * main : (tile + 1) * main]
                out[group * main : (group + 1) * main, lanes(tile)] = value
            ends.append(arrived[column, group, tiles * main :].astype(jnp.float32))
        for tile in range(tiles):
            at = slice(tile // 2 * 2 * rest, (tile // 2 + 1) * 2 * rest)
            pairs = []
            for group in range(0, groups, 2):
                even, odd = ends[group][at], ends[group + 1][at]
                if tile % 2 == 0:
                    pairs.append(jnp.where(lower, even, odd))
                else:
                    pairs.append(pltpu.roll(jnp.where(lower, odd, even), rest, 0))
            value = jnp.concatenate(pairs, axis=0).astype(jnp.bfloat16)
            out[groups * main :, lanes(tile)] = value


def spread_body(main, rest, info, *refs):
    ins, out = refs[:-1], refs[-1]
    split, groups = out.shape[:2]
    tiles = ins[0].shape[1] // LANES
    lower = upper_half(rest) == 0
    for offset, rows in enumerate(ins):
        column = lax.rem(info[0] + offset, split)
        ends = rows[groups * main :].astype(jnp.float32)
        for group in range(groups):
            for tile in range(tiles):
                value = rows[group * main : (group + 1) * main, lanes(tile)]
                out[column, group, tile * main : (tile + 1) * main] = value
            mine = ends[group // 2 * 2 * rest : (group // 2 + 1) * 2 * rest]
            last = []
            for tile in range(0, tiles, 2):
                here = mine[:, lanes(tile)]
                after = pltpu.roll(mine[:, lanes(min(tile + 1, tiles - 1))], rest, 0)
                low, high = (here, after) if group % 2 == 0 else (after, here)
                last.append(jnp.where(lower, low, high))
            value = jnp.concatenate(last, axis=0).astype(jnp.bfloat16)
            out[column, group, tiles * main :] = value


def hidden_body(part, own, up, down, out):
    half = up.shape[1]
    for block in range(half // 256):
        at = block * 256
        sums = (
            own[:, part * half + at : part * half + at + 256]
            + up[:, at : at + 256].astype(jnp.float32)
            + down[:, at : at + 256].astype(jnp.float32)
        )
        gate, raised = sums[:, :128], sums[:, 128:]
        value = gate / (1.0 + jnp.exp(-gate)) * raised
        out[:, block * 128 : (block + 1) * 128] = value.astype(jnp.bfloat16)


def chosen_rows(main, place_main, place_rest, returned, piece):
    groups = returned.shape[1]
    tiles = place_rest.shape[0] // LANES
    whole = [
        jnp.concatenate(
            [returned[piece, group, tile * main : (tile + 1) * main] for group in range(groups)],
            axis=0,
        )
        for tile in range(tiles)
    ]
    chosen = jnp.dot(
        place_main[...], jnp.concatenate(whole, axis=1), preferred_element_type=jnp.float32
    )
    ends = [returned[piece, group, tiles * main :] for group in range(groups)]
    others = jnp.dot(
        place_rest[...], jnp.concatenate(ends, axis=0), preferred_element_type=jnp.float32
    )
    return chosen + jnp.concatenate([others[lanes(tile)] for tile in range(tiles)], axis=1)


def part_body(split, main, n_streams, start, info, *refs):
    streams = refs[:n_streams]
    place_main, weight, place_rest, returned, out = refs[n_streams:]
    width = out.shape[2]
    total = streams[0].shape[1] // split
    for piece in range(split):
        chosen = chosen_rows(main, place_main, place_rest, returned, piece)
        base = stream_piece(info, streams, piece, start, width, total)
        out[piece] = (base + chosen * weight[...]).astype(jnp.bfloat16)


def last_body(split, main, n_streams, n_before, info, *refs):
    streams, before = refs[:n_streams], refs[n_streams : n_streams + n_before]
    place_main, weight, place_rest, returned, out = refs[n_streams + n_before :]
    total = out.shape[2] // split
    for piece in range(split):
        low = piece * total
        for part in before:
            out[0, :, low : low + part.shape[2]] = part[piece]
            low += part.shape[2]
        chosen = chosen_rows(main, place_main, place_rest, returned, piece)
        base = stream_piece(info, streams, piece, 0, total, total)
        value = (base + chosen * weight[...]).astype(jnp.bfloat16)
        out[1, :, piece * total : (piece + 1) * total] = value


def per_device(tokens, entering, norm_gain, gate_up, down_proj, expert_ids, gate_weights):
    split = lax.axis_size("z")
    groups = lax.axis_size("y")
    row, place = lax.axis_index("y"), lax.axis_index("z")
    info = jnp.stack([place, lax.axis_index("segment"), row]).astype(jnp.int32)
    tok_rows, model_width = entering.shape
    slot_cap = 9 * tok_rows // (8 * groups)
    main = slot_cap // TILE * TILE
    rest = slot_cap - main
    block_rows = main + 2 * rest
    chunk_rows = groups * slot_cap
    piece_width = model_width // split
    hidden_width = down_proj.shape[2]
    half = hidden_width
    far = split // 2
    bf16, f32 = jnp.bfloat16, jnp.float32

    flat_ids = expert_ids[0].reshape(tok_rows)
    member = (flat_ids[:, None] == jnp.arange(groups, dtype=jnp.int32)[None, :]).astype(jnp.int32)
    slot_of = jnp.sum((jnp.cumsum(member, axis=0) - 1) * member, axis=1)
    block_places = jnp.arange(groups * block_rows, dtype=jnp.int32)
    places = flat_ids * block_rows + slot_of
    again = jnp.where(slot_of < main, places, places + rest)
    pick = (block_places[:, None] == places[None, :]) | (block_places[:, None] == again[None, :])
    pick = pick.astype(bf16)
    main_rows = jnp.arange(groups * main, dtype=jnp.int32)
    origin = jnp.where(slot_of < main, flat_ids * main + slot_of, -1)
    place_main = (origin[:, None] == main_rows[None, :]).astype(bf16)

    def place_rest(width):
        tiles = width // LANES
        end_rows = (tiles + 1) // 2 * 2 * rest
        tile = jnp.arange(tiles, dtype=jnp.int32)[:, None]
        at = flat_ids * end_rows + slot_of - main
        at = at[None, :] + tile // 2 * 2 * rest + (tile + row) % 2 * rest
        at = jnp.where(slot_of[None, :] < main, -1, at).reshape(tiles * tok_rows)
        rows = jnp.arange(groups * end_rows, dtype=jnp.int32)
        return (at[:, None] == rows[None, :]).astype(bf16)

    token_weight = gate_weights[0]
    weights_in = gate_up[0, 0].reshape(piece_width, 2 * hidden_width)
    weights_out = down_proj[0, 0]
    pick_flops = 2 * groups * block_rows * tok_rows * model_width

    def expert_blocks(streams, parts):
        sent_rows = packed_rows(main, rest, piece_width)
        outgoing = local_call(
            functools.partial(sending_body, split, main, rest, len(streams)),
            jax.ShapeDtypeStruct((split, groups, sent_rows, LANES), bf16),
            (info, *streams, norm_gain, pick),
            pick_flops,
            1,
        )
        arrived = exchanged(outgoing.reshape(split * groups, sent_rows, LANES))
        arrived = local_call(
            functools.partial(gathered_body, main, rest),
            [jax.ShapeDtypeStruct((chunk_rows, piece_width), bf16)] * split,
            (info, arrived.reshape(split, groups, sent_rows, LANES)),
            0,
            1,
        )

        def partial_sums(offset):
            return jnp.dot(arrived[offset % split], weights_in, preferred_element_type=f32)

        opposite = partial_sums(far).astype(bf16)
        low_up, high_down = opposite[:, :half], opposite[:, half:]
        high_up = low_down = None
        for step in range(far - 1, 0, -1):
            low_up = shifted(low_up, "z", 1)
            high_down = shifted(high_down, "z", -1)
            if high_up is not None:
                high_up = shifted(high_up, "z", 1)
                low_down = shifted(low_down, "z", -1)
            ahead, behind = partial_sums(step), partial_sums(-step)
            low_up = (low_up.astype(f32) + ahead[:, :half]).astype(bf16)
            high_down = (high_down.astype(f32) + behind[:, half:]).astype(bf16)
            if high_up is None:
                high_up = ahead[:, half:].astype(bf16)
                low_down = behind[:, :half].astype(bf16)
            else:
                high_up = (high_up.astype(f32) + ahead[:, half:]).astype(bf16)
                low_down = (low_down.astype(f32) + behind[:, :half]).astype(bf16)
        low_up, high_up = shifted(low_up, "z", 1), shifted(high_up, "z", 1)
        low_down, high_down = shifted(low_down, "z", -1), shifted(high_down, "z", -1)
        own = partial_sums(0)
        low, high = (
            local_call(
                functools.partial(hidden_body, part),
                jax.ShapeDtypeStruct((chunk_rows, hidden_width // 2), bf16),
                (own, up, down),
                4 * chunk_rows * hidden_width,
            )
            for part, (up, down) in enumerate(((low_up, low_down), (high_up, high_down)))
        )

        hidden = [None] * split
        hidden[0] = jnp.concatenate([low, high], axis=1)
        low_up = low_down = low
        high_up = high_down = high
        for step in range(1, far):
            low_up, high_up = shifted(low_up, "z", 1), shifted(high_up, "z", 1)
            high_down, low_down = shifted(high_down, "z", -1), shifted(low_down, "z", -1)
            hidden[split - step] = jnp.concatenate([low_up, high_up], axis=1)
            hidden[step] = jnp.concatenate([low_down, high_down], axis=1)
        low_up, high_down = shifted(low_up, "z", 1), shifted(high_down, "z", -1)
        hidden[far] = jnp.concatenate([low_up, high_down], axis=1)
        results = []
        for start, width in parts:
            wanted = weights_out[:, start : start + width]
            blocks = [
                jnp.dot(rows, wanted, preferred_element_type=f32).astype(bf16) for rows in hidden
            ]
            given_rows = packed_rows(main, rest, width)
            blocks = local_call(
                functools.partial(spread_body, main, rest),
                jax.ShapeDtypeStruct((split, groups, given_rows, LANES), bf16),
                (info, *blocks),
                0,
                1,
            )
            returned = exchanged(blocks.reshape(split * groups, given_rows, LANES))
            results.append(returned.reshape(split, groups, given_rows, LANES))
        return results

    first_streams = (tokens[0],)
    first_parts = ((0, 512), (512, piece_width - 512))
    last_parts = ((0, piece_width),)
    first, passed = [], []
    for (start, width), returned in zip(first_parts, expert_blocks(first_streams, first_parts)):
        first.append(
            local_call(
                functools.partial(part_body, split, main, len(first_streams), start),
                jax.ShapeDtypeStruct((split, tok_rows, width), bf16),
                (info, *first_streams, place_main, token_weight, place_rest(width), returned),
                pick_flops,
                1,
            )
        )
        passed.append(passed_along(first[-1], "segment", 1))
    second_streams = (entering, *passed)
    (returned,) = expert_blocks(second_streams, last_parts)
    results = local_call(
        functools.partial(last_body, split, main, len(second_streams), len(first)),
        jax.ShapeDtypeStruct((2, tok_rows, model_width), bf16),
        (
            info,
            *second_streams,
            *first,
            place_main,
            token_weight,
            place_rest(piece_width),
            returned,
        ),
        pick_flops,
        1,
    )
    return results[:, None]


def solution(mesh):
    segments, experts = mesh.devices.shape
    split = 8
    fine = Mesh(mesh.devices.reshape(segments, experts // split, split), ("segment", "y", "z"))
    both = ("y", "z")
    in_specs = (
        P("segment", both, None),
        P(both, None),
        P("segment", None),
        P("segment", both, None, None, None, None),
        P("segment", both, None, None),
        P("segment", both, None),
        P("segment", both, None),
    )
    out_specs = P(None, "segment", both, None)
    return jax.shard_map(
        per_device, mesh=fine, in_specs=in_specs, out_specs=out_specs, check_vma=False
    )
```

```python
import functools

import jax
import jax.numpy as jnp
from jax import lax
from jax.experimental import pallas as pl
from jax.experimental.pallas import tpu as pltpu
from jax.sharding import Mesh, PartitionSpec as P

EPSILON = 1e-06
TILE = 16
LANES = 128
VMEM_BYTES = 40 * 2**20
BOTH = ("z", "y")


def shifted(value, axis, by):
    count = lax.axis_size(axis)
    return lax.ppermute(value, axis, [(i, (i + by) % count) for i in range(count)])


def passed_along(shard, axis, by):
    count = lax.axis_size(axis)
    pairs = [(i, i + by) for i in range(count) if 0 <= i + by < count]
    return lax.ppermute(shard, axis, pairs)


def packed_rows(main, rest, width):
    tiles = width // LANES
    return tiles * main + (tiles + 1) // 2 * 2 * rest


def lanes(tile):
    return slice(tile * LANES, (tile + 1) * LANES)


def upper_half(rest):
    return lax.broadcasted_iota(jnp.int32, (2 * rest, LANES), 0) // rest


def exchanged(blocks):
    return lax.all_to_all(blocks, BOTH, split_axis=0, concat_axis=0, tiled=True)


def local_call(body, out_shape, operands, flops, scalars=0):
    vmem = pl.BlockSpec(memory_space=pltpu.VMEM)
    smem = pl.BlockSpec(memory_space=pltpu.SMEM)
    moved = sum(v.size * v.dtype.itemsize for v in (*operands, *jax.tree.leaves(out_shape)))
    return pl.pallas_call(
        body,
        out_shape=out_shape,
        in_specs=[smem] * scalars + [vmem] * (len(operands) - scalars),
        out_specs=jax.tree.map(lambda _: vmem, out_shape),
        compiler_params=pltpu.CompilerParams(vmem_limit_bytes=VMEM_BYTES),
        cost_estimate=pl.CostEstimate(flops=flops, bytes_accessed=moved, transcendentals=0),
    )(*operands)


def stream_piece(info, streams, piece, start, width, total):
    at = piece * total + start
    whole = streams[0][:, at : at + width].astype(jnp.float32)
    if len(streams) == 1:
        return whole
    parts, low = [], 0
    for part in streams[1:]:
        size = part.shape[2]
        if low < start + width and start < low + size:
            left, right = max(start - low, 0), min(start + width - low, size)
            parts.append(part[piece, :, left:right].astype(jnp.float32))
        low += size
    passed = parts[0] if len(parts) == 1 else jnp.concatenate(parts, axis=1)
    first = (jnp.zeros((1, 1), jnp.int32) + info[1]) == 0
    return jnp.where(first, whole, passed)


def pick_rows(ids, groups, main, rest):
    block_rows = main + 2 * rest
    tok_rows = ids.shape[1]
    member = lax.broadcasted_iota(jnp.int32, (8, tok_rows), 0) == ids
    member = jnp.where(member, 1.0, 0.0)
    before = lax.broadcasted_iota(jnp.int32, (tok_rows, tok_rows), 0)
    after = lax.broadcasted_iota(jnp.int32, (tok_rows, tok_rows), 1)
    upto = jnp.where(before <= after, 1.0, 0.0).astype(jnp.bfloat16)
    counts = jnp.dot(member.astype(jnp.bfloat16), upto, preferred_element_type=jnp.float32)
    slot_of = jnp.sum(counts * member, axis=0, keepdims=True).astype(jnp.int32) - 1
    places = ids * block_rows + slot_of
    again = jnp.where(slot_of < main, places, places + rest)
    rows = lax.broadcasted_iota(jnp.int32, (groups * block_rows, tok_rows), 0)
    return jnp.where((rows == places) | (rows == again), 1.0, 0.0).astype(jnp.bfloat16)


def sending_body(split, main, rest, n_streams, info, *refs):
    streams, (gain, ids), out = refs[:n_streams], refs[n_streams : n_streams + 2], refs[-1]
    width = gain.shape[1] // split
    tiles = width // LANES
    groups = out.shape[1]
    block_rows = main + 2 * rest
    pick = pick_rows(ids[...], groups, main, rest)
    own_half = upper_half(rest) == lax.rem(info[2], 2)
    squares = 0.0
    for piece in range(split):
        values = stream_piece(info, streams, piece, 0, width, width)
        squares = squares + jnp.sum(values * values, axis=1, keepdims=True)
    scale = lax.rsqrt(squares / gain.shape[1] + EPSILON)
    for piece in range(split):
        values = stream_piece(info, streams, piece, 0, width, width)
        normed = values * scale * gain[:, piece * width : (piece + 1) * width]
        rows = jnp.dot(pick, normed.astype(jnp.bfloat16), preferred_element_type=jnp.float32)
        for group in range(groups):
            block = rows[group * block_rows : (group + 1) * block_rows]
            for tile in range(tiles):
                value = block[:main, lanes(tile)].astype(jnp.bfloat16)
                out[piece, group, tile * main : (tile + 1) * main] = value
            last = []
            for tile in range(0, tiles, 2):
                here = block[main:, lanes(tile)]
                after = block[main:, lanes(min(tile + 1, tiles - 1))]
                last.append(jnp.where(own_half, here, after))
            value = jnp.concatenate(last, axis=0).astype(jnp.bfloat16)
            out[piece, group, tiles * main :] = value


def gathered_body(main, rest, info, arrived, *outs):
    split, groups = arrived.shape[:2]
    tiles = outs[0].shape[1] // LANES
    lower = upper_half(rest) == 0
    for offset, out in enumerate(outs):
        column = lax.rem(info[0] + offset, split)
        ends = []
        for group in range(groups):
            for tile in range(tiles):
                value = arrived[column, group, tile * main : (tile + 1) * main]
                out[group * main : (group + 1) * main, lanes(tile)] = value
            ends.append(arrived[column, group, tiles * main :].astype(jnp.float32))
        for tile in range(tiles):
            at = slice(tile // 2 * 2 * rest, (tile // 2 + 1) * 2 * rest)
            pairs = []
            for group in range(0, groups, 2):
                even, odd = ends[group][at], ends[group + 1][at]
                if tile % 2 == 0:
                    pairs.append(jnp.where(lower, even, odd))
                else:
                    pairs.append(pltpu.roll(jnp.where(lower, odd, even), rest, 0))
            value = jnp.concatenate(pairs, axis=0).astype(jnp.bfloat16)
            out[groups * main :, lanes(tile)] = value


def spread_body(main, rest, info, *refs):
    ins, out = refs[:-1], refs[-1]
    split, groups = out.shape[:2]
    tiles = ins[0].shape[1] // LANES
    lower = upper_half(rest) == 0
    for offset, rows in enumerate(ins):
        column = lax.rem(info[0] + offset, split)
        ends = rows[groups * main :].astype(jnp.float32)
        for group in range(groups):
            for tile in range(tiles):
                value = rows[group * main : (group + 1) * main, lanes(tile)]
                out[column, group, tile * main : (tile + 1) * main] = value
            mine = ends[group // 2 * 2 * rest : (group // 2 + 1) * 2 * rest]
            last = []
            for tile in range(0, tiles, 2):
                here = mine[:, lanes(tile)]
                after = pltpu.roll(mine[:, lanes(min(tile + 1, tiles - 1))], rest, 0)
                low, high = (here, after) if group % 2 == 0 else (after, here)
                last.append(jnp.where(lower, low, high))
            value = jnp.concatenate(last, axis=0).astype(jnp.bfloat16)
            out[column, group, tiles * main :] = value


def hidden_body(part, own, up, down, out):
    half = up.shape[1]
    for block in range(half // 256):
        at = block * 256
        sums = (
            own[:, part * half + at : part * half + at + 256]
            + up[:, at : at + 256].astype(jnp.float32)
            + down[:, at : at + 256].astype(jnp.float32)
        )
        gate, raised = sums[:, :128], sums[:, 128:]
        value = gate / (1.0 + jnp.exp(-gate)) * raised
        out[:, block * 128 : (block + 1) * 128] = value.astype(jnp.bfloat16)


def chosen_rows(main, place_main, place_rest, returned, piece):
    groups = returned.shape[1]
    tiles = place_rest.shape[0] // LANES
    whole = [
        jnp.concatenate(
            [returned[piece, group, tile * main : (tile + 1) * main] for group in range(groups)],
            axis=0,
        )
        for tile in range(tiles)
    ]
    chosen = jnp.dot(
        place_main[...], jnp.concatenate(whole, axis=1), preferred_element_type=jnp.float32
    )
    ends = [returned[piece, group, tiles * main :] for group in range(groups)]
    others = jnp.dot(
        place_rest[...], jnp.concatenate(ends, axis=0), preferred_element_type=jnp.float32
    )
    return chosen + jnp.concatenate([others[lanes(tile)] for tile in range(tiles)], axis=1)


def part_body(split, main, n_streams, start, info, *refs):
    streams = refs[:n_streams]
    place_main, weight, place_rest, returned, out = refs[n_streams:]
    width = out.shape[2]
    total = streams[0].shape[1] // split
    for piece in range(split):
        chosen = chosen_rows(main, place_main, place_rest, returned, piece)
        base = stream_piece(info, streams, piece, start, width, total)
        out[piece] = (base + chosen * weight[...]).astype(jnp.bfloat16)


def kept_body(split, *refs):
    before, out = refs[:-1], refs[-1]
    total = out.shape[2] // split
    for piece in range(split):
        low = piece * total
        for part in before:
            out[0, :, low : low + part.shape[2]] = part[piece]
            low += part.shape[2]


def last_body(split, main, n_streams, info, *refs):
    streams = refs[:n_streams]
    place_main, weight, place_rest, returned, _, out = refs[n_streams:]
    total = out.shape[2] // split
    for piece in range(split):
        chosen = chosen_rows(main, place_main, place_rest, returned, piece)
        base = stream_piece(info, streams, piece, 0, total, total)
        value = (base + chosen * weight[...]).astype(jnp.bfloat16)
        out[0, :, piece * total : (piece + 1) * total] = value


def half_call(body, tick, shape, operands, flops, onto=None):
    vmem = pl.BlockSpec(memory_space=pltpu.VMEM)
    specs = [vmem] * len(operands)
    aliases = {}
    if onto is not None:
        specs = [pl.BlockSpec(memory_space=pltpu.SMEM), *specs[1:], pl.BlockSpec(memory_space=pl.ANY)]
        aliases = {len(operands): 0}
        operands = (*operands, onto)
    moved = shape.size * shape.dtype.itemsize
    return pl.pallas_call(
        body,
        grid=(1,),
        out_shape=shape,
        in_specs=specs,
        out_specs=pl.BlockSpec((1, *shape.shape[1:]), lambda step: (tick, 0, 0)),
        input_output_aliases=aliases,
        compiler_params=pltpu.CompilerParams(vmem_limit_bytes=VMEM_BYTES),
        cost_estimate=pl.CostEstimate(flops=flops, bytes_accessed=moved, transcendentals=0),
    )(*operands)


def per_device(tokens, entering, norm_gain, gate_up, down_proj, expert_ids, gate_weights):
    split = lax.axis_size("z")
    groups = lax.axis_size("y")
    row, place = lax.axis_index("y"), lax.axis_index("z")
    info = jnp.stack([place, lax.axis_index("segment"), row]).astype(jnp.int32)
    tok_rows, model_width = entering.shape
    slot_cap = 9 * tok_rows // (8 * groups)
    main = slot_cap // TILE * TILE
    rest = slot_cap - main
    block_rows = main + 2 * rest
    chunk_rows = groups * slot_cap
    piece_width = model_width // split
    hidden_width = down_proj.shape[2]
    half = hidden_width
    far = split // 2
    bf16, f32 = jnp.bfloat16, jnp.float32

    flat_ids = expert_ids[0].reshape(tok_rows)
    member = (flat_ids[:, None] == jnp.arange(groups, dtype=jnp.int32)[None, :]).astype(jnp.int32)
    slot_of = jnp.sum((jnp.cumsum(member, axis=0) - 1) * member, axis=1)
    main_rows = jnp.arange(groups * main, dtype=jnp.int32)
    origin = jnp.where(slot_of < main, flat_ids * main + slot_of, -1)
    place_main = (origin[:, None] == main_rows[None, :]).astype(bf16)

    def place_rest(width):
        tiles = width // LANES
        end_rows = (tiles + 1) // 2 * 2 * rest
        tile = jnp.arange(tiles, dtype=jnp.int32)[:, None]
        at = flat_ids * end_rows + slot_of - main
        at = at[None, :] + tile // 2 * 2 * rest + (tile + row) % 2 * rest
        at = jnp.where(slot_of[None, :] < main, -1, at).reshape(tiles * tok_rows)
        rows = jnp.arange(groups * end_rows, dtype=jnp.int32)
        return (at[:, None] == rows[None, :]).astype(bf16)

    token_weight = gate_weights[0]
    weights_in = gate_up[0, 0].reshape(piece_width, 2 * hidden_width)
    weights_out = down_proj[0, 0]
    pick_flops = 2 * groups * block_rows * tok_rows * model_width

    def expert_blocks(streams, parts):
        sent_rows = packed_rows(main, rest, piece_width)
        outgoing = local_call(
            functools.partial(sending_body, split, main, rest, len(streams)),
            jax.ShapeDtypeStruct((split, groups, sent_rows, LANES), bf16),
            (info, *streams, norm_gain, flat_ids.reshape(1, tok_rows)),
            pick_flops,
            1,
        )
        arrived = exchanged(outgoing.reshape(split * groups, sent_rows, LANES))
        arrived = local_call(
            functools.partial(gathered_body, main, rest),
            [jax.ShapeDtypeStruct((chunk_rows, piece_width), bf16)] * split,
            (info, arrived.reshape(split, groups, sent_rows, LANES)),
            0,
            1,
        )

        def partial_sums(offset):
            return jnp.dot(arrived[offset % split], weights_in, preferred_element_type=f32)

        opposite = partial_sums(far).astype(bf16)
        low_up, high_down = opposite[:, :half], opposite[:, half:]
        high_up = low_down = None
        for step in range(far - 1, 0, -1):
            low_up = shifted(low_up, "z", 1)
            high_down = shifted(high_down, "z", -1)
            if high_up is not None:
                high_up = shifted(high_up, "z", 1)
                low_down = shifted(low_down, "z", -1)
            ahead, behind = partial_sums(step), partial_sums(-step)
            low_up = (low_up.astype(f32) + ahead[:, :half]).astype(bf16)
            high_down = (high_down.astype(f32) + behind[:, half:]).astype(bf16)
            if high_up is None:
                high_up = ahead[:, half:].astype(bf16)
                low_down = behind[:, :half].astype(bf16)
            else:
                high_up = (high_up.astype(f32) + ahead[:, half:]).astype(bf16)
                low_down = (low_down.astype(f32) + behind[:, :half]).astype(bf16)
        low_up, high_up = shifted(low_up, "z", 1), shifted(high_up, "z", 1)
        low_down, high_down = shifted(low_down, "z", -1), shifted(high_down, "z", -1)
        own = partial_sums(0)
        low, high = (
            local_call(
                functools.partial(hidden_body, part),
                jax.ShapeDtypeStruct((chunk_rows, hidden_width // 2), bf16),
                (own, up, down),
                4 * chunk_rows * hidden_width,
            )
            for part, (up, down) in enumerate(((low_up, low_down), (high_up, high_down)))
        )

        hidden = [None] * split
        hidden[0] = jnp.concatenate([low, high], axis=1)
        low_up = low_down = low
        high_up = high_down = high
        for step in range(1, far):
            low_up, high_up = shifted(low_up, "z", 1), shifted(high_up, "z", 1)
            high_down, low_down = shifted(high_down, "z", -1), shifted(low_down, "z", -1)
            hidden[split - step] = jnp.concatenate([low_up, high_up], axis=1)
            hidden[step] = jnp.concatenate([low_down, high_down], axis=1)
        low_up, high_down = shifted(low_up, "z", 1), shifted(high_down, "z", -1)
        hidden[far] = jnp.concatenate([low_up, high_down], axis=1)
        results = []
        for start, width in parts:
            wanted = weights_out[:, start : start + width]
            blocks = [
                jnp.dot(rows, wanted, preferred_element_type=f32).astype(bf16) for rows in hidden
            ]
            given_rows = packed_rows(main, rest, width)
            blocks = local_call(
                functools.partial(spread_body, main, rest),
                jax.ShapeDtypeStruct((split, groups, given_rows, LANES), bf16),
                (info, *blocks),
                0,
                1,
            )
            returned = exchanged(blocks.reshape(split * groups, given_rows, LANES))
            results.append(returned.reshape(split, groups, given_rows, LANES))
        return results

    first_streams = (tokens[0],)
    first_parts = ((0, 512), (512, piece_width - 512))
    last_parts = ((0, piece_width),)
    first, passed = [], []
    for (start, width), returned in zip(first_parts, expert_blocks(first_streams, first_parts)):
        first.append(
            local_call(
                functools.partial(part_body, split, main, len(first_streams), start),
                jax.ShapeDtypeStruct((split, tok_rows, width), bf16),
                (info, *first_streams, place_main, token_weight, place_rest(width), returned),
                pick_flops,
                1,
            )
        )
        passed.append(passed_along(first[-1], "segment", 1))
    second_streams = (entering, *passed)
    (returned,) = expert_blocks(second_streams, last_parts)
    whole = jax.ShapeDtypeStruct((2, tok_rows, model_width), bf16)
    kept = half_call(functools.partial(kept_body, split), 0, whole, tuple(first), 0)
    results = half_call(
        functools.partial(last_body, split, main, len(second_streams)),
        1,
        whole,
        (
            info,
            *second_streams,
            place_main,
            token_weight,
            place_rest(piece_width),
            returned,
        ),
        pick_flops,
        kept,
    )
    return results[:, None]


def solution(mesh):
    segments, experts = mesh.devices.shape
    split = 8
    fine = Mesh(mesh.devices.reshape(segments, experts // split, split), ("segment", "y", "z"))
    both = ("y", "z")
    in_specs = (
        P("segment", both, None),
        P(both, None),
        P("segment", None),
        P("segment", both, None, None, None, None),
        P("segment", both, None, None),
        P("segment", both, None),
        P("segment", both, None),
    )
    out_specs = P(None, "segment", both, None)
    return jax.shard_map(
        per_device, mesh=fine, in_specs=in_specs, out_specs=out_specs, check_vma=False
    )
```

```python
import functools

import jax
import jax.numpy as jnp
from jax import lax
from jax.experimental import pallas as pl
from jax.experimental.pallas import tpu as pltpu
from jax.sharding import Mesh, PartitionSpec as P

EPSILON = 1e-06
TILE = 16
LANES = 128
VMEM_BYTES = 40 * 2**20
BOTH = ("z", "y")


def shifted(value, axis, by):
    count = lax.axis_size(axis)
    return lax.ppermute(value, axis, [(i, (i + by) % count) for i in range(count)])


def passed_along(shard, axis, by):
    count = lax.axis_size(axis)
    pairs = [(i, i + by) for i in range(count) if 0 <= i + by < count]
    return lax.ppermute(shard, axis, pairs)


def packed_rows(main, rest, width):
    tiles = width // LANES
    return tiles * main + end_groups(tiles) * 2 * rest


def end_groups(tiles):
    return (tiles + 3) // 4 * 2


def lanes(tile):
    return slice(tile * LANES, (tile + 1) * LANES)


def upper_half(rest):
    return lax.broadcasted_iota(jnp.int32, (2 * rest, LANES), 0) // rest


def exchanged(blocks):
    return lax.all_to_all(blocks, BOTH, split_axis=0, concat_axis=0, tiled=True)


def local_call(body, out_shape, operands, flops, scalars=0):
    vmem = pl.BlockSpec(memory_space=pltpu.VMEM)
    smem = pl.BlockSpec(memory_space=pltpu.SMEM)
    moved = sum(v.size * v.dtype.itemsize for v in (*operands, *jax.tree.leaves(out_shape)))
    return pl.pallas_call(
        body,
        out_shape=out_shape,
        in_specs=[smem] * scalars + [vmem] * (len(operands) - scalars),
        out_specs=jax.tree.map(lambda _: vmem, out_shape),
        compiler_params=pltpu.CompilerParams(vmem_limit_bytes=VMEM_BYTES),
        cost_estimate=pl.CostEstimate(flops=flops, bytes_accessed=moved, transcendentals=0),
    )(*operands)


def stream_piece(info, streams, piece, start, width, total):
    at = piece * total + start
    whole = streams[0][:, at : at + width].astype(jnp.float32)
    if len(streams) == 1:
        return whole
    parts, low = [], 0
    for part in streams[1:]:
        size = part.shape[2]
        if low < start + width and start < low + size:
            left, right = max(start - low, 0), min(start + width - low, size)
            parts.append(part[piece, :, left:right].astype(jnp.float32))
        low += size
    passed = parts[0] if len(parts) == 1 else jnp.concatenate(parts, axis=1)
    first = (jnp.zeros((1, 1), jnp.int32) + info[1]) == 0
    return jnp.where(first, whole, passed)


def pick_rows(ids, groups, main, rest):
    block_rows = main + 2 * rest
    tok_rows = ids.shape[1]
    member = lax.broadcasted_iota(jnp.int32, (8, tok_rows), 0) == ids
    member = jnp.where(member, 1.0, 0.0)
    before = lax.broadcasted_iota(jnp.int32, (tok_rows, tok_rows), 0)
    after = lax.broadcasted_iota(jnp.int32, (tok_rows, tok_rows), 1)
    upto = jnp.where(before <= after, 1.0, 0.0).astype(jnp.bfloat16)
    counts = jnp.dot(member.astype(jnp.bfloat16), upto, preferred_element_type=jnp.float32)
    slot_of = jnp.sum(counts * member, axis=0, keepdims=True).astype(jnp.int32) - 1
    places = ids * block_rows + slot_of
    again = jnp.where(slot_of < main, places, places + rest)
    rows = lax.broadcasted_iota(jnp.int32, (groups * block_rows, tok_rows), 0)
    return jnp.where((rows == places) | (rows == again), 1.0, 0.0).astype(jnp.bfloat16)


def sending_body(split, main, rest, n_streams, info, *refs):
    streams, (gain, ids), out = refs[:n_streams], refs[n_streams : n_streams + 2], refs[-1]
    width = gain.shape[1] // split
    tiles = width // LANES
    groups = out.shape[1]
    block_rows = main + 2 * rest
    pick = pick_rows(ids[...], groups, main, rest)
    own_half = upper_half(rest) == lax.rem(info[2], 2)
    squares = 0.0
    for piece in range(split):
        values = stream_piece(info, streams, piece, 0, width, width)
        squares = squares + jnp.sum(values * values, axis=1, keepdims=True)
    scale = lax.rsqrt(squares / gain.shape[1] + EPSILON)
    for piece in range(split):
        values = stream_piece(info, streams, piece, 0, width, width)
        normed = values * scale * gain[:, piece * width : (piece + 1) * width]
        rows = jnp.dot(pick, normed.astype(jnp.bfloat16), preferred_element_type=jnp.float32)
        for group in range(groups):
            block = rows[group * block_rows : (group + 1) * block_rows]
            for tile in range(tiles):
                value = block[:main, lanes(tile)].astype(jnp.bfloat16)
                out[piece, group, tile * main : (tile + 1) * main] = value
            last = []
            for tile in range(0, tiles, 2):
                here = block[main:, lanes(tile)]
                after = block[main:, lanes(min(tile + 1, tiles - 1))]
                last.append(jnp.where(own_half, here, after))
            value = jnp.concatenate(last, axis=0).astype(jnp.bfloat16)
            out[piece, group, tiles * main :] = value


def gathered_body(main, rest, info, arrived, *outs):
    split, groups = arrived.shape[:2]
    tiles = outs[0].shape[1] // LANES
    lower = upper_half(rest) == 0
    for offset, out in enumerate(outs):
        column = lax.rem(info[0] + offset, split)
        ends = []
        for group in range(groups):
            for tile in range(tiles):
                value = arrived[column, group, tile * main : (tile + 1) * main]
                out[group * main : (group + 1) * main, lanes(tile)] = value
            ends.append(arrived[column, group, tiles * main :].astype(jnp.float32))
        for tile in range(tiles):
            at = slice(tile // 2 * 2 * rest, (tile // 2 + 1) * 2 * rest)
            pairs = []
            for group in range(0, groups, 2):
                even, odd = ends[group][at], ends[group + 1][at]
                if tile % 2 == 0:
                    pairs.append(jnp.where(lower, even, odd))
                else:
                    pairs.append(pltpu.roll(jnp.where(lower, odd, even), rest, 0))
            value = jnp.concatenate(pairs, axis=0).astype(jnp.bfloat16)
            out[groups * main :, lanes(tile)] = value


def spread_body(main, rest, info, *refs):
    ins, out = refs[:-1], refs[-1]
    split, groups = out.shape[:2]
    tiles = ins[0].shape[1] // LANES
    lower = upper_half(rest) == 0
    for offset, rows in enumerate(ins):
        column = lax.rem(info[0] + offset, split)
        ends = rows[groups * main :].astype(jnp.float32)
        for group in range(groups):
            for tile in range(tiles):
                value = rows[group * main : (group + 1) * main, lanes(tile)]
                out[column, group, tile * main : (tile + 1) * main] = value
            mine = ends[group // 2 * 2 * rest : (group // 2 + 1) * 2 * rest]
            last = []
            for tile in range(0, 2 * end_groups(tiles), 2):
                here = mine[:, lanes(min(tile, tiles - 1))]
                after = pltpu.roll(mine[:, lanes(min(tile + 1, tiles - 1))], rest, 0)
                low, high = (here, after) if group % 2 == 0 else (after, here)
                last.append(jnp.where(lower, low, high))
            value = jnp.concatenate(last, axis=0).astype(jnp.bfloat16)
            out[column, group, tiles * main :] = value


def hidden_body(part, own, up, down, out):
    half = up.shape[1]
    for block in range(half // 256):
        at = block * 256
        sums = (
            own[:, part * half + at : part * half + at + 256]
            + up[:, at : at + 256].astype(jnp.float32)
            + down[:, at : at + 256].astype(jnp.float32)
        )
        gate, raised = sums[:, :128], sums[:, 128:]
        value = gate / (1.0 + jnp.exp(-gate)) * raised
        out[:, block * 128 : (block + 1) * 128] = value.astype(jnp.bfloat16)


def chosen_rows(main, place_main, place_rest, returned, piece):
    groups = returned.shape[1]
    tiles = place_rest.shape[0] // LANES
    whole = [
        jnp.concatenate(
            [returned[piece, group, tile * main : (tile + 1) * main] for group in range(groups)],
            axis=0,
        )
        for tile in range(tiles)
    ]
    chosen = jnp.dot(
        place_main[...], jnp.concatenate(whole, axis=1), preferred_element_type=jnp.float32
    )
    ends = [returned[piece, group, tiles * main :] for group in range(groups)]
    others = jnp.dot(
        place_rest[...], jnp.concatenate(ends, axis=0), preferred_element_type=jnp.float32
    )
    return chosen + jnp.concatenate([others[lanes(tile)] for tile in range(tiles)], axis=1)


def part_body(split, main, n_streams, start, info, *refs):
    streams = refs[:n_streams]
    place_main, weight, place_rest, returned, out = refs[n_streams:]
    width = out.shape[2]
    total = streams[0].shape[1] // split
    for piece in range(split):
        chosen = chosen_rows(main, place_main, place_rest, returned, piece)
        base = stream_piece(info, streams, piece, start, width, total)
        out[piece] = (base + chosen * weight[...]).astype(jnp.bfloat16)


def kept_body(split, *refs):
    before, out = refs[:-1], refs[-1]
    total = out.shape[2] // split
    for piece in range(split):
        low = piece * total
        for part in before:
            out[0, :, low : low + part.shape[2]] = part[piece]
            low += part.shape[2]


def last_body(split, main, n_streams, info, *refs):
    streams = refs[:n_streams]
    place_main, weight, place_rest, returned, _, out = refs[n_streams:]
    total = out.shape[2] // split
    for piece in range(split):
        chosen = chosen_rows(main, place_main, place_rest, returned, piece)
        base = stream_piece(info, streams, piece, 0, total, total)
        value = (base + chosen * weight[...]).astype(jnp.bfloat16)
        out[0, :, piece * total : (piece + 1) * total] = value


def half_call(body, tick, shape, operands, flops, onto=None):
    vmem = pl.BlockSpec(memory_space=pltpu.VMEM)
    specs = [vmem] * len(operands)
    aliases = {}
    if onto is not None:
        specs = [pl.BlockSpec(memory_space=pltpu.SMEM), *specs[1:], pl.BlockSpec(memory_space=pl.ANY)]
        aliases = {len(operands): 0}
        operands = (*operands, onto)
    moved = shape.size * shape.dtype.itemsize
    return pl.pallas_call(
        body,
        grid=(1,),
        out_shape=shape,
        in_specs=specs,
        out_specs=pl.BlockSpec((1, *shape.shape[1:]), lambda step: (tick, 0, 0)),
        input_output_aliases=aliases,
        compiler_params=pltpu.CompilerParams(vmem_limit_bytes=VMEM_BYTES),
        cost_estimate=pl.CostEstimate(flops=flops, bytes_accessed=moved, transcendentals=0),
    )(*operands)


def per_device(tokens, entering, norm_gain, gate_up, down_proj, expert_ids, gate_weights):
    split = lax.axis_size("z")
    groups = lax.axis_size("y")
    row, place = lax.axis_index("y"), lax.axis_index("z")
    info = jnp.stack([place, lax.axis_index("segment"), row]).astype(jnp.int32)
    tok_rows, model_width = entering.shape
    slot_cap = 9 * tok_rows // (8 * groups)
    main = slot_cap // TILE * TILE
    rest = slot_cap - main
    block_rows = main + 2 * rest
    chunk_rows = groups * slot_cap
    piece_width = model_width // split
    hidden_width = down_proj.shape[2]
    half = hidden_width
    far = split // 2
    bf16, f32 = jnp.bfloat16, jnp.float32

    flat_ids = expert_ids[0].reshape(tok_rows)
    member = (flat_ids[:, None] == jnp.arange(groups, dtype=jnp.int32)[None, :]).astype(jnp.int32)
    slot_of = jnp.sum((jnp.cumsum(member, axis=0) - 1) * member, axis=1)
    main_rows = jnp.arange(groups * main, dtype=jnp.int32)
    origin = jnp.where(slot_of < main, flat_ids * main + slot_of, -1)
    place_main = (origin[:, None] == main_rows[None, :]).astype(bf16)

    def place_rest(width):
        tiles = width // LANES
        end_rows = end_groups(tiles) * 2 * rest
        tile = jnp.arange(tiles, dtype=jnp.int32)[:, None]
        at = flat_ids * end_rows + slot_of - main
        at = at[None, :] + tile // 2 * 2 * rest + (tile + row) % 2 * rest
        at = jnp.where(slot_of[None, :] < main, -1, at).reshape(tiles * tok_rows)
        rows = jnp.arange(groups * end_rows, dtype=jnp.int32)
        return (at[:, None] == rows[None, :]).astype(bf16)

    token_weight = gate_weights[0]
    weights_in = gate_up[0, 0].reshape(piece_width, 2 * hidden_width)
    weights_out = down_proj[0, 0]
    pick_flops = 2 * groups * block_rows * tok_rows * model_width

    def expert_blocks(streams, parts, finished):
        sent_rows = packed_rows(main, rest, piece_width)
        outgoing = local_call(
            functools.partial(sending_body, split, main, rest, len(streams)),
            jax.ShapeDtypeStruct((split, groups, sent_rows, LANES), bf16),
            (info, *streams, norm_gain, flat_ids.reshape(1, tok_rows)),
            pick_flops,
            1,
        )
        arrived = exchanged(outgoing.reshape(split * groups, sent_rows, LANES))
        arrived = local_call(
            functools.partial(gathered_body, main, rest),
            [jax.ShapeDtypeStruct((chunk_rows, piece_width), bf16)] * split,
            (info, arrived.reshape(split, groups, sent_rows, LANES)),
            0,
            1,
        )

        def partial_sums(offset):
            return jnp.dot(arrived[offset % split], weights_in, preferred_element_type=f32)

        opposite = partial_sums(far).astype(bf16)
        low_up, high_down = opposite[:, :half], opposite[:, half:]
        high_up = low_down = None
        for step in range(far - 1, 0, -1):
            low_up = shifted(low_up, "z", 1)
            high_down = shifted(high_down, "z", -1)
            if high_up is not None:
                high_up = shifted(high_up, "z", 1)
                low_down = shifted(low_down, "z", -1)
            ahead, behind = partial_sums(step), partial_sums(-step)
            low_up = (low_up.astype(f32) + ahead[:, :half]).astype(bf16)
            high_down = (high_down.astype(f32) + behind[:, half:]).astype(bf16)
            if high_up is None:
                high_up = ahead[:, half:].astype(bf16)
                low_down = behind[:, :half].astype(bf16)
            else:
                high_up = (high_up.astype(f32) + ahead[:, half:]).astype(bf16)
                low_down = (low_down.astype(f32) + behind[:, :half]).astype(bf16)
        low_up, high_up = shifted(low_up, "z", 1), shifted(high_up, "z", 1)
        low_down, high_down = shifted(low_down, "z", -1), shifted(high_down, "z", -1)
        own = partial_sums(0)
        low, high = (
            local_call(
                functools.partial(hidden_body, part),
                jax.ShapeDtypeStruct((chunk_rows, hidden_width // 2), bf16),
                (own, up, down),
                4 * chunk_rows * hidden_width,
            )
            for part, (up, down) in enumerate(((low_up, low_down), (high_up, high_down)))
        )

        hidden = [None] * split
        hidden[0] = jnp.concatenate([low, high], axis=1)
        low_up = low_down = low
        high_up = high_down = high
        for step in range(1, far):
            low_up, high_up = shifted(low_up, "z", 1), shifted(high_up, "z", 1)
            high_down, low_down = shifted(high_down, "z", -1), shifted(low_down, "z", -1)
            hidden[split - step] = jnp.concatenate([low_up, high_up], axis=1)
            hidden[step] = jnp.concatenate([low_down, high_down], axis=1)
        low_up, high_down = shifted(low_up, "z", 1), shifted(high_down, "z", -1)
        hidden[far] = jnp.concatenate([low_up, high_down], axis=1)
        results = []
        for start, width in parts:
            wanted = weights_out[:, start : start + width]
            blocks = [
                jnp.dot(rows, wanted, preferred_element_type=f32).astype(bf16) for rows in hidden
            ]
            given_rows = packed_rows(main, rest, width)
            blocks = local_call(
                functools.partial(spread_body, main, rest),
                jax.ShapeDtypeStruct((split, groups, given_rows, LANES), bf16),
                (info, *blocks),
                0,
                1,
            )
            if results:
                blocks = lax.optimization_barrier((blocks, results[-1]))[0]
            returned = exchanged(blocks.reshape(split * groups, given_rows, LANES))
            results.append(
                finished(start, width, returned.reshape(split, groups, given_rows, LANES))
            )
        return results

    first_streams = (tokens[0],)
    first_parts = ((0, 640), (640, piece_width - 640))
    last_parts = ((0, piece_width),)

    def first_part(start, width, returned):
        return local_call(
            functools.partial(part_body, split, main, len(first_streams), start),
            jax.ShapeDtypeStruct((split, tok_rows, width), bf16),
            (info, *first_streams, place_main, token_weight, place_rest(width), returned),
            pick_flops,
            1,
        )

    first = expert_blocks(first_streams, first_parts, first_part)
    passed = [passed_along(part, "segment", 1) for part in first]
    second_streams = (entering, *passed)
    (returned,) = expert_blocks(second_streams, last_parts, lambda start, width, blocks: blocks)
    whole = jax.ShapeDtypeStruct((2, tok_rows, model_width), bf16)
    kept = half_call(functools.partial(kept_body, split), 0, whole, tuple(first), 0)
    results = half_call(
        functools.partial(last_body, split, main, len(second_streams)),
        1,
        whole,
        (
            info,
            *second_streams,
            place_main,
            token_weight,
            place_rest(piece_width),
            returned,
        ),
        pick_flops,
        kept,
    )
    return results[:, None]


def solution(mesh):
    segments, experts = mesh.devices.shape
    split = 8
    fine = Mesh(mesh.devices.reshape(segments, experts // split, split), ("segment", "y", "z"))
    both = ("y", "z")
    in_specs = (
        P("segment", both, None),
        P(both, None),
        P("segment", None),
        P("segment", both, None, None, None, None),
        P("segment", both, None, None),
        P("segment", both, None),
        P("segment", both, None),
    )
    out_specs = P(None, "segment", both, None)
    return jax.shard_map(
        per_device, mesh=fine, in_specs=in_specs, out_specs=out_specs, check_vma=False
    )
```
